256 devices in a mesh: section: 16 (over z, x_hi), peer: 16 (over y, x_lo, core).
Axes of the slice: x: 4 (x_hi: 2, x_lo: 2; x = x_hi * 2 + x_lo), y: 4, z: 8, core: 2. Of those that a mesh axis runs over, the one named last changes fastest.
Arguments:
- carried: bfloat16 [16, 16, 64, 5120], P('section', 'peer'), may hold values from -60 to 60
- pending: bfloat16 [16, 16, 64, 5120], P('section', 'peer'), may hold values from -6 to 6
- stashed_inputs: bfloat16 [16, 16, 4, 64, 5120], P('section', 'peer'), may hold values from -60 to 60
- fresh_batches: bfloat16 [3, 16, 64, 5120], P(None, 'peer'), may hold values from -60 to 60
- cotangent: bfloat16 [4, 16, 64, 5120], P(None, 'peer'), may hold values from -6 to 6
- norm_gain: float32 [16, 5120], P('section'), may hold values from 0.1 to 1.9
- w_down: bfloat16 [16, 5120, 256], P('section', 'peer'), may hold values from -0.078125 to 0.078125
- w_up: bfloat16 [16, 256, 5120], P('section', None, 'peer'), may hold values from -0.375 to 0.375
- forward_route: int32 [3, 15, 16], replicated, may hold values from 0 to 15, each once within a row
- backward_route: int32 [3, 15, 16], replicated, may hold values from 0 to 15, each once within a row
Outputs:
- outgoing: bfloat16 [16, 16, 64, 5120], P('section', 'peer')
- returning: bfloat16 [16, 16, 64, 5120], P('section', 'peer')
- grad_down: float32 [16, 5120, 256], P('section', 'peer')
- grad_up: float32 [16, 256, 5120], P('section', None, 'peer')
The draws below stay inside these ranges and needn't reach their ends.
Inputs may be any that keep to these rules, and one draw needn't show every extreme that they name: `forward_route`: each row along the last dimension names each of the 16 peers once. `backward_route`: each row along the last dimension names each of the 16 peers once.
All inputs are finite; a program needn't handle non-finite values.
Results may differ from the reference program's by a relative error of at most 0.023.
Values may be sent and summed in bfloat16 or wider, within the bound.
A program may use at most 128 MiB of HBM per device.

```python
import math
import jax
import jax.numpy as jnp
from jax import lax

D = 5120
R = 256
TOK = 64
TICKS = 4
SECTIONS = 16
PEERS = 16


def apply_scales(base_values, scale_key, shape_list):
    scales = jnp.exp(jax.random.uniform(scale_key, tuple(shape_list[:-1]) + (1,), jnp.float32, 0.0, math.log(10.0)))
    return base_values * scales


def draw_carried(key, part):
    key = jax.random.fold_in(key, 11)
    base_key, scale_key = jax.random.split(key, 2)
    shape_list = (SECTIONS, PEERS, TOK, D)
    base_values = jnp.clip(jax.random.normal(base_key, shape_list, jnp.float32), -6.0, 6.0)
    return apply_scales(base_values, scale_key, shape_list).astype(jnp.bfloat16)


def draw_stashed_inputs(key, part):
    key = jax.random.fold_in(key, 23)
    base_key, scale_key = jax.random.split(key, 2)
    shape_list = (SECTIONS, PEERS, TICKS, TOK, D)
    base_values = jnp.clip(jax.random.normal(base_key, shape_list, jnp.float32), -6.0, 6.0)
    return apply_scales(base_values, scale_key, shape_list).astype(jnp.bfloat16)


def draw_fresh_batches(key, part):
    key = jax.random.fold_in(key, 37)
    base_key, scale_key = jax.random.split(key, 2)
    shape_list = (TICKS - 1, PEERS, TOK, D)
    base_values = jnp.clip(jax.random.normal(base_key, shape_list, jnp.float32), -6.0, 6.0)
    return apply_scales(base_values, scale_key, shape_list).astype(jnp.bfloat16)


def block_levels(rng, shape, cuts, least, high):
    gain, own = 1.0, jax.random.fold_in(rng, 6)
    for dim, shards_of in cuts:
        heights = jnp.exp(jax.random.uniform(jax.random.fold_in(own, dim), (shards_of,), jnp.float32, least / len(cuts), high / len(cuts)))
        gain = gain * jnp.repeat(heights, shape[dim] // shards_of).reshape([-1 if axis == dim else 1 for axis in range(len(shape))])
    return gain


def gaussian(rng, extent, deviation, bound, pieces=(), dtype=jnp.bfloat16):
    level = block_levels(rng, extent, pieces, -0.22, 0.18) if pieces else 1.0
    values = jax.random.normal(rng, extent, jnp.float32) * deviation * level
    return jnp.minimum(jnp.maximum(values, -bound), bound).astype(dtype)


def setup_inputs(seed: int = 0) -> dict:
    key_of = jax.random.split(jax.random.key(seed), 11)
    carried = draw_carried(jax.random.fold_in(key_of[10], 71), 0)
    pending = gaussian(key_of[1], (SECTIONS, PEERS, TOK, D), 1.0, 6.0, ((0, 16), (1, 16)))
    stashed_inputs = draw_stashed_inputs(jax.random.fold_in(key_of[10], 71), 0)
    fresh_batches = draw_fresh_batches(jax.random.fold_in(key_of[10], 71), 0)
    cotangent = gaussian(key_of[4], (TICKS, PEERS, TOK, D), 1.0, 6.0, ((1, 16),))
    norm_gain = jnp.clip(1.0 + 0.18 * jax.random.normal(key_of[5], (SECTIONS, D), jnp.float32), 0.1, 1.9)
    w_down = gaussian(key_of[6], (SECTIONS, D, R), D ** -0.5, 0.078125, ((0, 16), (1, 16)))
    w_up = gaussian(key_of[7], (SECTIONS, R, D), R ** -0.5, 0.375, ((0, 16), (2, 16)))
    forward_route = jax.vmap(lambda own: jax.random.permutation(own, PEERS))(jax.random.split(key_of[8], (TICKS - 1) * (SECTIONS - 1))).reshape((TICKS - 1, SECTIONS - 1, PEERS)).astype(jnp.int32)
    backward_route = jax.vmap(lambda own: jax.random.permutation(own, PEERS))(jax.random.split(key_of[9], (TICKS - 1) * (SECTIONS - 1))).reshape((TICKS - 1, SECTIONS - 1, PEERS)).astype(jnp.int32)
    return dict(carried=carried, pending=pending, stashed_inputs=stashed_inputs, fresh_batches=fresh_batches, cotangent=cotangent, norm_gain=norm_gain, w_down=w_down, w_up=w_up, forward_route=forward_route, backward_route=backward_route)


NORM_EPS = 1e-05

def norm_parts(rows_in, gain_row):
    input_float = rows_in.astype(jnp.float32)
    norm_scale = lax.rsqrt(lax.optimization_barrier(jnp.mean(input_float * input_float, axis=-1, keepdims=True)) + NORM_EPS)
    normed = (input_float * norm_scale * gain_row).astype(jnp.bfloat16)
    return (input_float, norm_scale, normed)

def section_forward(rows_in, gain_row, down_matrix, up_matrix):
    input_float, norm_scale, normed = norm_parts(rows_in, gain_row)
    latent = jnp.dot(normed, down_matrix, preferred_element_type=jnp.float32)
    hidden = (latent * jax.nn.sigmoid(latent)).astype(jnp.bfloat16)
    result = input_float + jnp.dot(hidden, up_matrix, preferred_element_type=jnp.float32)
    return result.astype(jnp.bfloat16)

def section_backward(rows_in, output_grad, gain_row, down_matrix, up_matrix):
    input_float, norm_scale, normed = norm_parts(rows_in, gain_row)
    latent = jnp.dot(normed, down_matrix, preferred_element_type=jnp.float32)
    sigmoid_latent = jax.nn.sigmoid(latent)
    hidden = (latent * sigmoid_latent).astype(jnp.bfloat16)
    hidden_grad = lax.dot_general(output_grad, up_matrix, (((1,), (1,)), ((), ())), preferred_element_type=jnp.float32)
    latent_grad = (hidden_grad * sigmoid_latent * (1.0 + latent * (1.0 - sigmoid_latent))).astype(jnp.bfloat16)
    normed_grad = lax.dot_general(latent_grad, down_matrix, (((1,), (1,)), ((), ())), preferred_element_type=jnp.float32)
    scaled = normed_grad * gain_row
    cubed = norm_scale * norm_scale * norm_scale
    input_grad = output_grad.astype(jnp.float32) + norm_scale * scaled - input_float * cubed * lax.optimization_barrier(jnp.mean(scaled * input_float, axis=-1, keepdims=True))
    return (input_grad.astype(jnp.bfloat16), normed, latent_grad, hidden)

def permute_rows(block, matching):
    return jnp.zeros_like(block).at[matching].set(block)

def one_section(section_items):
    activations, backward_inputs, output_grads, gain_row, down_matrix, up_matrix = section_items
    flat_acts = activations.reshape(-1, activations.shape[-1])
    flat_inputs = backward_inputs.reshape(-1, activations.shape[-1])
    flat_grads = output_grads.reshape(-1, activations.shape[-1])
    result = section_forward(flat_acts, gain_row, down_matrix, up_matrix)
    input_grad, normed, latent_grad, hidden = section_backward(flat_inputs, flat_grads, gain_row, down_matrix, up_matrix)
    down_part = lax.dot_general(normed, latent_grad, (((0,), (0,)), ((), ())), preferred_element_type=jnp.float32)
    up_part = lax.dot_general(hidden, flat_grads, (((0,), (0,)), ((), ())), preferred_element_type=jnp.float32)
    return (result.reshape(activations.shape), input_grad.reshape(activations.shape), down_part, up_part)

def reference(carried, pending, stashed_inputs, fresh_batches, cotangent, norm_gain, w_down, w_up, forward_route, backward_route):
    activations = carried
    lower_grads = pending[:-1]
    down_total = jnp.zeros((SECTIONS, D, R), jnp.float32)
    up_total = jnp.zeros((SECTIONS, R, D), jnp.float32)
    outgoing = carried
    returning = pending
    for tick_index in range(TICKS):
        if tick_index > 0:
            arrived = jax.vmap(permute_rows)(outgoing[:-1], forward_route[tick_index - 1])
            activations = jnp.concatenate([fresh_batches[tick_index - 1][None], arrived], axis=0)
            lower_grads = jax.vmap(permute_rows)(returning[1:], backward_route[tick_index - 1])
        output_grads = jnp.concatenate([lower_grads, cotangent[tick_index][None]], axis=0)
        backward_inputs = jnp.concatenate([stashed_inputs[:-1, :, tick_index], activations[-1:]], axis=0)
        outgoing, returning, down_parts, up_parts = lax.map(one_section, (activations, backward_inputs, output_grads, norm_gain, w_down, w_up))
        down_total = down_total + down_parts
        up_total = up_total + up_parts
    return (outgoing, returning, down_total, up_total)
```

```python
import functools

import jax
import jax.numpy as jnp
from jax import lax
from jax.experimental import pallas as pl
from jax.experimental.pallas import tpu as pltpu
from jax.sharding import PartitionSpec as P

MESH = pl.DeviceIdType.MESH
NORM_EPS = 1e-05
TICKS = 4
XS = 4
YS = 4
PEERS = 16
LANES = 128


def high_low(value):
    high = value.astype(jnp.bfloat16).astype(jnp.float32)
    return high, value - high


def kernel(
    planes,
    width,
    inverse,
    carried,
    pending,
    stash,
    fresh,
    cotangent,
    w_down,
    w_up,
    out_ref,
    ret_ref,
    grad_ref,
    x_now,
    v_now,
    u_all,
    fresh_all,
    x_in,
    v_in,
    x_out,
    v_out,
    part_send,
    part_recv,
    rows_all,
    down_all,
    up_all,
    grad_sum,
    grad_send,
    grad_recv,
    spread_send,
    spread_recv,
    part_sems,
    rows_sems,
    hop_send,
    hop_recv,
    last_send,
    last_recv,
):
    section = lax.axis_index("section")
    peer = lax.axis_index("peer")
    z, x_hi = section // 2, section % 2
    y, x_lo, core = peer // 4, (peer // 2) % 2, peer % 2
    x = 2 * x_hi + x_lo
    mine = 2 * z + core
    tokens, columns = x_now.shape[1], x_now.shape[2]
    shard = w_down.shape[0]
    rank = w_down.shape[1]
    rows = PEERS * tokens
    share = rows // YS
    home = core == x_hi
    away = core != x_hi
    is_first = mine == 0
    is_last = mine == 2 * planes - 1
    sends_last = section == 2 * planes - 1

    def place(zz, xx, yy, cc):
        return (2 * zz + xx // 2, 4 * yy + 2 * (xx % 2) + cc)

    def remote(src, dst, send_sem, recv_sem, device):
        pltpu.make_async_remote_copy(
            src_ref=src,
            dst_ref=dst,
            send_sem=send_sem,
            recv_sem=recv_sem,
            device_id=device,
            device_id_type=MESH,
        ).start()

    def settle(ref, sem):
        pltpu.make_async_copy(ref, ref, sem).wait()

    barrier = pltpu.get_barrier_semaphore()
    z_up, z_down = (z + 1) % planes, (z + planes - 1) % planes

    @pl.loop(1, 32)
    def _(i):
        other = (x * 8 + y * 2 + core + i) % 32
        pl.semaphore_signal(
            barrier, inc=1, device_id=place(z, other // 8, (other // 2) % 4, other % 2), device_id_type=MESH
        )

    for zz in (z_up, z_down):
        pl.semaphore_signal(barrier, inc=1, device_id=place(zz, x, y, 1 - core), device_id_type=MESH)
    pl.semaphore_wait(barrier, 33)

    def spread(source, target, send_sem, recv_sem):
        def piece(xx, yy):
            return source.at[
                pl.ds(pl.multiple_of(xx * tokens, tokens), tokens),
                pl.ds(pl.multiple_of(yy * columns, LANES), columns),
            ]

        @pl.when(home)
        def _():
            pltpu.make_async_copy(piece(x, y), target.at[peer], recv_sem).start()

        @pl.when(away)
        def _():
            remote(piece(x, y), target.at[peer], send_sem, recv_sem, place(z, x, y, x_hi))

        @pl.loop(1, XS * YS)
        def _(i):
            xx, yy = (x + i // YS) % XS, (y + i) % YS
            remote(piece(xx, yy), target.at[peer], send_sem, recv_sem, place(z, xx, yy, x_hi))

    def spread_weight(source, target, send_sem, recv_sem):
        block = target.at[pl.ds(pl.multiple_of((2 * x_lo + core) * shard, 16), shard)]

        @pl.when(home)
        def _():
            pltpu.make_async_copy(source, block, recv_sem).start()

        @pl.when(away)
        def _():
            remote(source, block, send_sem, recv_sem, place(z, x, y, x_hi))

        @pl.loop(1, XS)
        def _(i):
            remote(source, block, send_sem, recv_sem, place(z, (x + i) % XS, y, x_hi))

    def settle_sent(ref, count, sem):
        @pl.when(home)
        def _():
            settle(ref.at[pl.ds(0, count - 1)], sem)

        @pl.when(away)
        def _():
            settle(ref.at[pl.ds(0, count)], sem)

    DOWN, CARRIED, UP, PENDING, FRESH, STASH = 0, 1, 2, 3, 4, 5

    def spread_stash(t):
        sems = (spread_send.at[STASH + t], spread_recv.at[STASH + t])

        @pl.when(sends_last)
        def _():
            spread(cotangent.at[t], u_all.at[t], *sems)

        @pl.when(jnp.logical_not(sends_last))
        def _():
            spread(stash.at[t], u_all.at[t], *sems)

    spread_weight(w_down, down_all, spread_send.at[DOWN], spread_recv.at[DOWN])
    spread(carried, x_now, spread_send.at[CARRIED], spread_recv.at[CARRIED])
    spread_weight(w_up, up_all, spread_send.at[UP], spread_recv.at[UP])
    spread(pending, v_now, spread_send.at[PENDING], spread_recv.at[PENDING])
    spread_stash(0)

    def fresh_piece(xx, yy):
        return fresh.at[
            :,
            pl.ds(pl.multiple_of(xx * tokens, tokens), tokens),
            pl.ds(pl.multiple_of(yy * columns, LANES), columns),
        ]

    @pl.when(z == 0)
    def _():
        sems = (spread_send.at[FRESH], spread_recv.at[FRESH])

        @pl.when(core == 0)
        def _():
            pltpu.make_async_copy(fresh_piece(x, y), fresh_all.at[:, peer], sems[1]).start()

        @pl.when(core == 1)
        def _():
            remote(fresh_piece(x, y), fresh_all.at[:, peer], *sems, place(z, x, y, 0))

        @pl.loop(1, 2 * YS)
        def _(i):
            xx, yy = 2 * x_hi + (x_lo + i // YS) % 2, (y + i) % YS
            remote(fresh_piece(xx, yy), fresh_all.at[:, peer], *sems, place(z, xx, yy, 0))

    lane = lax.broadcasted_iota(jnp.int32, (rows, LANES), 1)

    def in_lanes(lane, values):
        result = jnp.zeros(lane.shape, jnp.float32)
        for i, value in enumerate(values):
            result = jnp.where(lane == i, value, result)
        return result.astype(jnp.bfloat16)

    def flat(value):
        return value.reshape(rows, value.shape[-1])

    def square_sum(value):
        value = value.astype(jnp.float32)
        return jnp.sum(value * value, axis=-1, keepdims=True)

    def product(a, b, contract):
        return lax.dot_general(a, b, ((contract[:1], contract[1:]), ((), ())), preferred_element_type=jnp.float32)

    grad_sum[...] = jnp.zeros_like(grad_sum)

    for t in range(TICKS):
        if t > 0:
            settle(x_in[t - 1], hop_recv.at[0, t - 1])
            settle(v_in[t - 1], hop_recv.at[1, t - 1])

            @pl.when(is_first)
            def _():
                if t == 1:
                    settle(fresh_all, spread_recv.at[FRESH])
                x_now[...] = fresh_all[t - 1]

            @pl.when(jnp.logical_not(is_first))
            def _():
                for p in range(PEERS):
                    x_now[p] = x_in[t - 1][inverse[t - 1, p]]

            for p in range(PEERS):
                v_now[p] = v_in[t - 1][inverse[TICKS - 2 + t, p]]
        else:
            settle(down_all, spread_recv.at[DOWN])
            settle(x_now, spread_recv.at[CARRIED])
        x_rows = flat(x_now[...])
        part_send[t, :, :, 0:rank] = (
            product(x_rows, down_all[...], (1, 0)).astype(jnp.bfloat16).reshape(YS, share, rank)
        )
        if t == 0:
            settle(up_all, spread_recv.at[UP])
            settle(v_now, spread_recv.at[PENDING])
        settle(u_all.at[t], spread_recv.at[STASH + t])

        @pl.when(is_last)
        def _():
            v_now[...] = u_all[t]
            u_all[t] = x_now[...]

        part_send[t, :, :, rank : 2 * rank] = (
            product(flat(v_now[...]), up_all[...], (1, 0)).astype(jnp.bfloat16).reshape(YS, share, rank)
        )
        u_rows = flat(u_all[t])
        part_send[t, :, :, 2 * rank : 3 * rank] = (
            product(u_rows, down_all[...], (1, 0)).astype(jnp.bfloat16).reshape(YS, share, rank)
        )
        part_send[t, :, :, 3 * rank :] = in_lanes(
            lane, high_low(square_sum(x_rows)) + high_low(square_sum(u_rows))
        ).reshape(YS, share, LANES)

        for i in range(1, YS):
            yy = (y + i) % YS
            remote(
                part_send.at[t, yy],
                part_recv.at[t, i - 1],
                part_sems.at[0, t],
                part_sems.at[1, t],
                place(z, x, yy, core),
            )
        settle(part_recv.at[t], part_sems.at[1, t])
        total = part_send[t, y].astype(jnp.float32)
        for i in range(YS - 1):
            total = total + part_recv[t, i].astype(jnp.float32)
        extra = total[:, 3 * rank :]
        x_scale = lax.rsqrt((extra[:, 0:1] + extra[:, 1:2]) * (1.0 / width) + NORM_EPS)
        u_scale = lax.rsqrt((extra[:, 2:3] + extra[:, 3:4]) * (1.0 / width) + NORM_EPS)
        latent = total[:, 0:rank] * x_scale
        rows_all[t, y, :, 0:rank] = (latent * jax.nn.sigmoid(latent)).astype(jnp.bfloat16)
        latent = total[:, 2 * rank : 3 * rank] * u_scale
        sigmoid = jax.nn.sigmoid(latent)
        rows_all[t, y, :, 2 * rank : 3 * rank] = (latent * sigmoid).astype(jnp.bfloat16)
        latent_grad = total[:, rank : 2 * rank] * sigmoid * (1.0 + latent * (1.0 - sigmoid))
        rows_all[t, y, :, rank : 2 * rank] = (latent_grad * u_scale).astype(jnp.bfloat16)
        along = jnp.sum(latent_grad * latent, axis=-1, keepdims=True) * (u_scale * u_scale * (1.0 / width))
        rows_all[t, y, :, 3 * rank :] = in_lanes(lane[:share], high_low(along))
        for i in range(1, YS):
            remote(
                rows_all.at[t, y],
                rows_all.at[t, y],
                rows_sems.at[0, t],
                rows_sems.at[1, t],
                place(z, x, (y + i) % YS, core),
            )
        settle(rows_all.at[t, pl.ds(0, YS - 1)], rows_sems.at[1, t])

        hidden = flat(rows_all[t, :, :, 0:rank])
        latent_grad = flat(rows_all[t, :, :, rank : 2 * rank])
        extra = flat(rows_all[t, :, :, 3 * rank :]).astype(jnp.float32)
        along = extra[:, 0:1] + extra[:, 1:2]
        step = 2 * LANES
        for start in range(0, columns, step):
            cut = slice(start, start + step)
            result = flat(x_now[:, :, cut]).astype(jnp.float32) + product(hidden, up_all[cut, :], (1, 1))
            x_out[t, :, :, cut] = result.astype(jnp.bfloat16).reshape(PEERS, tokens, step)
        if t < TICKS - 1:
            remote(
                x_out.at[t],
                x_in[t],
                hop_send.at[0, t],
                hop_recv.at[0, t],
                place((z + core) % planes, x, y, 1 - core),
            )
        for start in range(0, columns, step):
            cut = slice(start, start + step)
            result = (
                flat(v_now[:, :, cut]).astype(jnp.float32)
                + product(latent_grad, down_all[cut, :], (1, 1))
                - flat(u_all[t, :, :, cut]).astype(jnp.float32) * along
            )
            v_out[t, :, :, cut] = result.astype(jnp.bfloat16).reshape(PEERS, tokens, step)
        if t < TICKS - 1:
            remote(
                v_out.at[t],
                v_in[t],
                hop_send.at[1, t],
                hop_recv.at[1, t],
                place((z + core + planes - 1) % planes, x, y, 1 - core),
            )
            spread_stash(t + 1)
        else:
            for k, (source, target) in enumerate(((x_out.at[t], out_ref), (v_out.at[t], ret_ref))):
                block = target.at[
                    pl.ds(pl.multiple_of(x * tokens, tokens), tokens),
                    pl.ds(pl.multiple_of(y * columns, LANES), columns),
                ]

                @pl.when(home)
                def _():
                    pltpu.make_async_copy(source.at[peer], block, last_recv.at[k]).start()

                @pl.when(away)
                def _():
                    remote(source.at[peer], block, last_send.at[k], last_recv.at[k], (mine, peer))

                @pl.loop(1, PEERS)
                def _(i):
                    q = (peer + i) % PEERS
                    remote(source.at[q], block, last_send.at[k], last_recv.at[k], (mine, q))

        hidden = flat(rows_all[t, :, :, 2 * rank : 3 * rank])
        for start in range(0, columns, step):
            cut = slice(start, start + step)
            grad_sum[0, cut, :] += product(flat(u_all[t, :, :, cut]), latent_grad, (0, 0))
            grad_sum[1, cut, :] += product(flat(v_now[:, :, cut]), hidden, (0, 0))

    for q in range(4):
        for k in range(2):
            grad_send[q, k] = grad_sum[k, q * shard : (q + 1) * shard, :].astype(jnp.bfloat16)
    own = 2 * x_lo + core

    @pl.when(home)
    def _():
        pltpu.make_async_copy(grad_send.at[own], grad_recv.at[x], last_recv.at[2]).start()

    @pl.when(away)
    def _():
        remote(grad_send.at[own], grad_recv.at[x], last_send.at[2], last_recv.at[2], (mine, peer))

    @pl.loop(1, 4)
    def _(i):
        q = (own + i) % 4
        remote(grad_send.at[q], grad_recv.at[x], last_send.at[2], last_recv.at[2], (mine, 4 * y + q))

    settle(grad_recv, last_recv.at[2])
    total = grad_recv[0].astype(jnp.float32)
    for i in range(1, XS):
        total = total + grad_recv[i].astype(jnp.float32)
    grad_ref[...] = total

    settle(out_ref, last_recv.at[0])
    settle(ret_ref, last_recv.at[1])

    for k in (DOWN, UP):
        settle_sent(grad_send.at[:, 0], 4, spread_send.at[k])
    for k in (CARRIED, PENDING, *range(STASH, STASH + TICKS)):
        settle_sent(x_now, PEERS, spread_send.at[k])
    for k in range(2):
        settle_sent(x_now, PEERS, last_send.at[k])
    settle_sent(grad_send, 4, last_send.at[2])

    @pl.when(z == 0)
    def _():
        @pl.when(core == 0)
        def _():
            settle(fresh_all.at[:, pl.ds(0, 2 * YS - 1)], spread_send.at[FRESH])

        @pl.when(core == 1)
        def _():
            settle(fresh_all.at[:, pl.ds(0, 2 * YS)], spread_send.at[FRESH])

    for t in range(TICKS):
        settle(part_recv.at[t], part_sems.at[0, t])
        settle(rows_all.at[t, pl.ds(0, YS - 1)], rows_sems.at[0, t])
        if t < TICKS - 1:
            settle(x_out.at[t], hop_send.at[0, t])
            settle(v_out.at[t], hop_send.at[1, t])


def shards(
    planes,
    carried,
    pending,
    stashed_inputs,
    fresh_batches,
    cotangent,
    norm_gain,
    w_down,
    w_up,
    forward_route,
    backward_route,
):
    section = lax.axis_index("section")
    peer = lax.axis_index("peer")
    row_count, width = carried.shape[2:]
    shard, rank = w_down.shape[1:]
    tokens, columns = row_count // XS, width // YS
    rows = PEERS * tokens
    share = rows // YS
    message = 3 * rank + LANES

    mine = 2 * (section // 2) + peer % 2
    boundaries = forward_route.shape[1]
    routes = jnp.concatenate(
        [
            lax.dynamic_index_in_dim(forward_route, jnp.clip(mine - 1, 0, boundaries - 1), 1, keepdims=False),
            lax.dynamic_index_in_dim(backward_route, jnp.clip(mine, 0, boundaries - 1), 1, keepdims=False),
        ]
    )
    places = jnp.arange(PEERS, dtype=jnp.int32)
    inverse = jnp.sum(jnp.where(routes[:, None, :] == places[None, :, None], places[None, None, :], 0), axis=2)

    gain = lax.dynamic_slice_in_dim(norm_gain[0], peer * shard, shard, 0)[:, None]
    down_gained = (w_down[0].astype(jnp.float32) * gain).astype(jnp.bfloat16)
    up_turned = w_up[0].T

    block = (PEERS, tokens, columns)
    bf16, f32 = jnp.bfloat16, jnp.float32
    dma = pltpu.SemaphoreType.DMA
    any_space = pl.BlockSpec(memory_space=pl.ANY)
    outgoing, returning, grads = pl.pallas_call(
        functools.partial(kernel, planes, width),
        out_shape=(
            jax.ShapeDtypeStruct((row_count, width), bf16),
            jax.ShapeDtypeStruct((row_count, width), bf16),
            jax.ShapeDtypeStruct((2, shard, rank), f32),
        ),
        in_specs=[pl.BlockSpec(memory_space=pltpu.SMEM)] + [any_space] * 7,
        out_specs=(any_space, any_space, pl.BlockSpec(memory_space=pltpu.VMEM)),
        scratch_shapes=[
            pltpu.VMEM(block, bf16),
            pltpu.VMEM(block, bf16),
            pltpu.VMEM((TICKS, *block), bf16),
            pltpu.VMEM((TICKS - 1, *block), bf16),
            (pltpu.VMEM(block, bf16),) * (TICKS - 1),
            (pltpu.VMEM(block, bf16),) * (TICKS - 1),
            pltpu.VMEM((TICKS, *block), bf16),
            pltpu.VMEM((TICKS, *block), bf16),
            pltpu.VMEM((TICKS, YS, share, message), bf16),
            pltpu.VMEM((TICKS, YS - 1, share, message), bf16),
            pltpu.VMEM((TICKS, YS, share, message), bf16),
            pltpu.VMEM((columns, rank), bf16),
            pltpu.VMEM((columns, rank), bf16),
            pltpu.VMEM((2, columns, rank), f32),
            pltpu.VMEM((4, 2, shard, rank), bf16),
            pltpu.VMEM((XS, 2, shard, rank), bf16),
            dma((5 + TICKS,)),
            dma((5 + TICKS,)),
            dma((2, TICKS)),
            dma((2, TICKS)),
            dma((2, TICKS - 1)),
            dma((2, TICKS - 1)),
            dma((3,)),
            dma((3,)),
        ],
        compiler_params=pltpu.CompilerParams(
            collective_id=0, has_side_effects=True, vmem_limit_bytes=52 * 1024 * 1024
        ),
    )(
        inverse,
        carried[0, 0],
        pending[0, 0],
        stashed_inputs[0, 0],
        fresh_batches[:, 0],
        cotangent[:, 0],
        down_gained,
        up_turned,
    )
    return (
        outgoing[None, None],
        returning[None, None],
        (grads[0] * gain)[None],
        grads[1].T[None],
    )


def solution(mesh):
    planes = mesh.shape["section"] // 2
    in_specs = (
        P("section", "peer", None, None),
        P("section", "peer", None, None),
        P("section", "peer", None, None, None),
        P(None, "peer", None, None),
        P(None, "peer", None, None),
        P("section", None),
        P("section", "peer", None),
        P("section", None, "peer"),
        P(),
        P(),
    )
    out_specs = (
        P("section", "peer", None, None),
        P("section", "peer", None, None),
        P("section", "peer", None),
        P("section", None, "peer"),
    )
    return jax.shard_map(
        functools.partial(shards, planes), mesh=mesh, in_specs=in_specs, out_specs=out_specs, check_vma=False
    )
```

```python
import functools

import jax
import jax.numpy as jnp
from jax import lax
from jax.experimental import pallas as pl
from jax.experimental.pallas import tpu as pltpu
from jax.sharding import PartitionSpec as P

MESH = pl.DeviceIdType.MESH
NORM_EPS = 1e-05
TICKS = 4
XS = 4
YS = 4
PEERS = 16
LANES = 128
STEP = 256
SPARE = 16

DOWN, CARRIED, UP, PENDING, FRESH, GAIN, STASH = 0, 1, 2, 3, 4, 5, 6
F_SUM, S_SUM, B_SUM, F_ROWS, S_ROWS, B_ROWS = range(6)


def iota(shape, dim):
    return lax.broadcasted_iota(jnp.int32, shape, dim)


def to_row(column, first, length):
    shape = (column.shape[0], length)
    return jnp.sum(jnp.where(iota(shape, 1) == iota(shape, 0) + first, column, 0.0), axis=0, keepdims=True)


def to_column(row, first, count):
    shape = (count, row.shape[1])
    return jnp.sum(jnp.where(iota(shape, 1) == iota(shape, 0) + first, row, 0.0), axis=1, keepdims=True)


def in_two(row):
    high = row.astype(jnp.bfloat16).astype(jnp.float32)
    shape = (SPARE, row.shape[1])
    sub = iota(shape, 0)
    return jnp.where(sub == 0, high, jnp.where(sub == 1, row - high, 0.0)).astype(jnp.bfloat16)


def product(a, b, left, right):
    return lax.dot_general(a, b, (((left,), (right,)), ((), ())), preferred_element_type=jnp.float32)


def kernel(
    planes,
    width,
    forward_route,
    backward_route,
    carried,
    pending,
    stash,
    fresh,
    cotangent,
    gain,
    w_down,
    w_up,
    out_ref,
    ret_ref,
    down_ref,
    up_ref,
    inverse,
    gain_row,
    w_up_here,
    w_up_turned,
    x_now,
    v_now,
    u_gained,
    u_all,
    fresh_all,
    x_in,
    v_in,
    x_out,
    v_out,
    f_send,
    f_recv,
    s_send,
    s_recv,
    b_send,
    b_recv,
    f_rows,
    s_rows,
    b_rows,
    down_all,
    up_all,
    grad_sum,
    grad_send,
    grad_recv,
    local_sem,
    spread_send,
    spread_recv,
    sum_send,
    sum_recv,
    hop_send,
    hop_recv,
    last_send,
    last_recv,
):
    section = lax.axis_index("section")
    peer = lax.axis_index("peer")
    z, x_hi = section // 2, section % 2
    y, x_lo, core = peer // 4, (peer // 2) % 2, peer % 2
    x = 2 * x_hi + x_lo
    mine = 2 * z + core
    tokens, columns = x_now.shape[1], x_now.shape[2]
    shard, rank = w_down.shape
    rows = PEERS * tokens
    share = rows // YS
    home = core == x_hi
    away = core != x_hi
    is_first = mine == 0
    is_last = mine == 2 * planes - 1
    sends_last = section == 2 * planes - 1

    def place(zz, xx, yy, cc):
        return (2 * zz + xx // 2, 4 * yy + 2 * (xx % 2) + cc)

    def remote(src, dst, send_sem, recv_sem, device):
        pltpu.make_async_remote_copy(
            src_ref=src,
            dst_ref=dst,
            send_sem=send_sem,
            recv_sem=recv_sem,
            device_id=device,
            device_id_type=MESH,
        ).start()

    def settle(ref, sem):
        pltpu.make_async_copy(ref, ref, sem).wait()

    pltpu.make_async_copy(w_up, w_up_here, local_sem).start()

    barrier = pltpu.get_barrier_semaphore()
    z_up, z_down = (z + 1) % planes, (z + planes - 1) % planes

    @pl.loop(1, 32)
    def _(i):
        other = (x * 8 + y * 2 + core + i) % 32
        pl.semaphore_signal(
            barrier, inc=1, device_id=place(z, other // 8, (other // 2) % 4, other % 2), device_id_type=MESH
        )

    for zz in (z_up, z_down):
        pl.semaphore_signal(barrier, inc=1, device_id=place(zz, x, y, 1 - core), device_id_type=MESH)
    pl.semaphore_wait(barrier, 33)

    def cut_of(ref, xx, yy):
        tok = pl.ds(pl.multiple_of(xx * tokens, tokens), tokens)
        col = pl.ds(pl.multiple_of(yy * columns, LANES), columns)
        return ref.at[tok, col] if len(ref.shape) == 2 else ref.at[:, tok, col]

    def spread(source, target, k):
        sems = (spread_send.at[k], spread_recv.at[k])

        @pl.when(home)
        def _():
            pltpu.make_async_copy(cut_of(source, x, y), target.at[peer], sems[1]).start()

        @pl.when(away)
        def _():
            remote(cut_of(source, x, y), target.at[peer], *sems, place(z, x, y, x_hi))

        @pl.loop(1, XS * YS)
        def _(i):
            xx, yy = (x + i // YS) % XS, (y + i) % YS
            remote(cut_of(source, xx, yy), target.at[peer], *sems, place(z, xx, yy, x_hi))

    def spread_weight(source, target, k):
        sems = (spread_send.at[k], spread_recv.at[k])
        block = target.at[pl.ds(pl.multiple_of((2 * x_lo + core) * shard, 16), shard)]

        @pl.when(home)
        def _():
            pltpu.make_async_copy(source, block, sems[1]).start()

        @pl.when(away)
        def _():
            remote(source, block, *sems, place(z, x, y, x_hi))

        @pl.loop(1, XS)
        def _(i):
            remote(source, block, *sems, place(z, (x + i) % XS, y, x_hi))

    def settle_sent(ref, count, sem):
        @pl.when(home)
        def _():
            settle(ref.at[pl.ds(0, count - 1)], sem)

        @pl.when(away)
        def _():
            settle(ref.at[pl.ds(0, count)], sem)

    def spread_stash(t):
        @pl.when(sends_last)
        def _():
            spread(cotangent.at[t], u_all.at[t], STASH + t)

        @pl.when(jnp.logical_not(sends_last))
        def _():
            spread(stash.at[t], u_all.at[t], STASH + t)

    gain_home = jnp.logical_and(home, x == 2 * x_lo + core)
    gain_cut = gain.at[:, pl.ds(pl.multiple_of(y * columns, LANES), columns)]

    @pl.when(gain_home)
    def _():
        pltpu.make_async_copy(gain_cut, gain_row, spread_recv.at[GAIN]).start()

    @pl.when(jnp.logical_not(gain_home))
    def _():
        remote(
            gain_cut, gain_row, spread_send.at[GAIN], spread_recv.at[GAIN], place(z, 2 * x_lo + core, y, x_hi)
        )

    spread_weight(w_down, down_all, DOWN)
    spread(carried, x_now, CARRIED)
    pltpu.make_async_copy(w_up, w_up_here, local_sem).wait()
    w_up_turned[...] = w_up_here[...].T
    spread_weight(w_up_turned, up_all, UP)
    spread_stash(0)
    spread(pending, v_now, PENDING)

    @pl.when(z == 0)
    def _():
        sems = (spread_send.at[FRESH], spread_recv.at[FRESH])
        target = fresh_all.at[:, peer]

        @pl.when(core == 0)
        def _():
            pltpu.make_async_copy(cut_of(fresh, x, y), target, sems[1]).start()

        @pl.when(core == 1)
        def _():
            remote(cut_of(fresh, x, y), target, *sems, place(z, x, y, 0))

        @pl.loop(1, 2 * YS)
        def _(i):
            xx, yy = 2 * x_hi + (x_lo + i // YS) % 2, (y + i) % YS
            remote(cut_of(fresh, xx, yy), target, *sems, place(z, xx, yy, 0))

    grad_sum[...] = jnp.zeros_like(grad_sum)

    boundary = (jnp.maximum(mine - 1, 0), jnp.minimum(mine, 2 * planes - 2))
    for t in range(TICKS - 1):
        for way, route in enumerate((forward_route, backward_route)):
            goes_to = [route[t, boundary[way], q] for q in range(PEERS)]

            @pl.loop(0, PEERS)
            def _(p):
                comes_from = 0
                for q in range(1, PEERS):
                    comes_from = jnp.where(goes_to[q] == p, q, comes_from)
                inverse[way * (TICKS - 1) + t, p] = comes_from

    def flat(value):
        return value.reshape(rows, value.shape[-1])

    def times_gain(value):
        return (value.astype(jnp.float32) * gain_row[...]).astype(jnp.bfloat16)

    def squares_row(value):
        value = value.astype(jnp.float32)
        return in_two(to_row(jnp.sum(value * value, axis=-1, keepdims=True), 0, rows))

    def send_sums(source, target, kind, t):
        for i in range(1, YS):
            yy = (y + i) % YS
            remote(
                source.at[t, yy],
                target.at[t, i - 1],
                sum_send.at[kind, t],
                sum_recv.at[kind, t],
                place(z, x, yy, core),
            )

    def take_sum(source, target, kind, t):
        settle(target.at[t], sum_recv.at[kind, t])
        total = source[t, y].astype(jnp.float32)
        for i in range(YS - 1):
            total = total + target[t, i].astype(jnp.float32)
        return total

    def send_rows(target, kind, t):
        for i in range(1, YS):
            remote(
                target.at[t, y],
                target.at[t, y],
                sum_send.at[kind, t],
                sum_recv.at[kind, t],
                place(z, x, (y + i) % YS, core),
            )

    def take_rows(target, kind, t):
        settle(target.at[t, pl.ds(0, YS - 1)], sum_recv.at[kind, t])

    def scale_of(total):
        squares = to_column(total[share : share + 1] + total[share + 1 : share + 2], y * share, share)
        return lax.rsqrt(squares * (1.0 / width) + NORM_EPS)

    def put_sums(target, t, value):
        target[t, :, 0:share, :] = value.astype(jnp.bfloat16).reshape(YS, share, rank)

    def put_squares(target, t, block):
        for yy in range(YS):
            target[t, yy, share:, :] = block

    def forward_first(t):
        if t == 0:
            settle(down_all, spread_recv.at[DOWN])
            settle(gain_row, spread_recv.at[GAIN])
            settle(x_now, spread_recv.at[CARRIED])
        else:
            settle(x_in[t - 1], hop_recv.at[0, t - 1])

            @pl.when(is_first)
            def _():
                if t == 1:
                    settle(fresh_all, spread_recv.at[FRESH])
                x_now[...] = fresh_all[t - 1]

            @pl.when(jnp.logical_not(is_first))
            def _():
                for p in range(PEERS):
                    x_now[p] = x_in[t - 1][inverse[t - 1, p]]

        x_rows = flat(x_now[...])
        put_sums(f_send, t, product(times_gain(x_rows), down_all[...], 1, 0))
        put_squares(f_send, t, squares_row(x_rows))
        send_sums(f_send, f_recv, F_SUM, t)

    def forward_second(t):
        total = take_sum(f_send, f_recv, F_SUM, t)
        scale = scale_of(total)
        latent = total[0:share] * scale
        f_rows[t, y] = (latent * jax.nn.sigmoid(latent)).astype(jnp.bfloat16)
        send_rows(f_rows, F_ROWS, t)
        return latent, scale

    def forward_third(t):
        if t == 0:
            settle(up_all, spread_recv.at[UP])
        take_rows(f_rows, F_ROWS, t)
        hidden = flat(f_rows[t])
        for start in range(0, columns, STEP):
            cut = slice(start, start + STEP)
            result = flat(x_now[:, :, cut]).astype(jnp.float32) + product(hidden, up_all[cut, :], 1, 1)
            x_out[t, :, :, cut] = result.astype(jnp.bfloat16).reshape(PEERS, tokens, STEP)
            if t < TICKS - 1:
                remote(
                    x_out.at[t, :, :, cut],
                    x_in[t].at[:, :, cut],
                    hop_send.at[0, t],
                    hop_recv.at[0, t],
                    place((z + core) % planes, x, y, 1 - core),
                )
        if t == TICKS - 1:
            to_peers(x_out.at[t], out_ref, 0)

    def stash_first(t):
        settle(u_all.at[t], spread_recv.at[STASH + t])
        u_rows = flat(u_all[t])
        u_gained[...] = times_gain(u_rows)
        put_sums(s_send, t, product(u_gained[...], down_all[...], 1, 0))
        put_squares(s_send, t, squares_row(u_rows))
        send_sums(s_send, s_recv, S_SUM, t)

    def stash_second(t):
        total = take_sum(s_send, s_recv, S_SUM, t)
        scale = scale_of(total)
        latent = total[0:share] * scale
        s_rows[t, y] = (latent * jax.nn.sigmoid(latent)).astype(jnp.bfloat16)
        send_rows(s_rows, S_ROWS, t)
        return latent, scale

    def backward_first(t):
        if t == 0:
            settle(v_now, spread_recv.at[PENDING])
        else:
            settle(v_in[t - 1], hop_recv.at[1, t - 1])
            for p in range(PEERS):
                v_now[p] = v_in[t - 1][inverse[TICKS - 2 + t, p]]

        @pl.when(is_last)
        def _():
            v_now[...] = u_all[t]
            u_all[t] = x_now[...]
            u_gained[...] = times_gain(flat(x_now[...]))

        put_sums(b_send, t, product(flat(v_now[...]), up_all[...], 1, 0))
        send_sums(b_send, b_recv, B_SUM, t)

    def backward_second(t, forward_latent, stash_latent):
        total = take_sum(b_send, b_recv, B_SUM, t)
        latent = jnp.where(is_last, forward_latent[0], stash_latent[0])
        scale = jnp.where(is_last, forward_latent[1], stash_latent[1])
        sigmoid = jax.nn.sigmoid(latent)
        latent_grad = total * sigmoid * (1.0 + latent * (1.0 - sigmoid))
        b_rows[t, y, 0:share, :] = (latent_grad * scale).astype(jnp.bfloat16)
        along = jnp.sum(latent_grad * latent, axis=-1, keepdims=True) * (scale * scale * (1.0 / width))
        b_rows[t, y, share:, :] = in_two(to_row(along, y * share, rows))
        send_rows(b_rows, B_ROWS, t)

    def backward_third(t):
        take_rows(b_rows, B_ROWS, t)
        latent_grad = flat(b_rows[t, :, 0:share, :])
        extra = b_rows[t, :, share:, :].astype(jnp.float32)
        along = to_column(jnp.sum(extra[:, 0:1] + extra[:, 1:2], axis=0), 0, rows)
        for start in range(0, columns, STEP):
            cut = slice(start, start + STEP)
            result = (
                flat(v_now[:, :, cut]).astype(jnp.float32)
                + product(latent_grad, down_all[cut, :], 1, 1) * gain_row[:, cut]
                - flat(u_all[t, :, :, cut]).astype(jnp.float32) * along
            )
            v_out[t, :, :, cut] = result.astype(jnp.bfloat16).reshape(PEERS, tokens, STEP)
            if t < TICKS - 1:
                remote(
                    v_out.at[t, :, :, cut],
                    v_in[t].at[:, :, cut],
                    hop_send.at[1, t],
                    hop_recv.at[1, t],
                    place((z + core + planes - 1) % planes, x, y, 1 - core),
                )
        if t == TICKS - 1:
            to_peers(v_out.at[t], ret_ref, 1)

    def to_peers(source, target, k):
        sems = (last_send.at[k], last_recv.at[k])
        block = cut_of(target, x, y)

        @pl.when(home)
        def _():
            pltpu.make_async_copy(source.at[peer], block, sems[1]).start()

        @pl.when(away)
        def _():
            remote(source.at[peer], block, *sems, (mine, peer))

        @pl.loop(1, PEERS)
        def _(i):
            q = (peer + i) % PEERS
            remote(source.at[q], block, *sems, (mine, q))

    def grad_up(t):
        take_rows(s_rows, S_ROWS, t)
        hidden = jnp.where(is_last, flat(f_rows[t]), flat(s_rows[t]))
        for start in range(0, columns, STEP):
            cut = slice(start, start + STEP)
            grad_sum[1, cut, :] += product(flat(v_now[:, :, cut]), hidden, 0, 0)

    def grad_down(t):
        latent_grad = flat(b_rows[t, :, 0:share, :])
        for start in range(0, columns, STEP):
            cut = slice(start, start + STEP)
            grad_sum[0, cut, :] += product(u_gained[:, cut], latent_grad, 0, 0)

    def to_owners(k):
        for q in range(4):
            grad_send[k, q] = grad_sum[k, q * shard : (q + 1) * shard, :].astype(jnp.bfloat16)
        sems = (last_send.at[2 + k], last_recv.at[2 + k])
        own = 2 * x_lo + core

        @pl.when(home)
        def _():
            pltpu.make_async_copy(grad_send.at[k, own], grad_recv.at[k, x], sems[1]).start()

        @pl.when(away)
        def _():
            remote(grad_send.at[k, own], grad_recv.at[k, x], *sems, (mine, peer))

        @pl.loop(1, 4)
        def _(i):
            q = (own + i) % 4
            remote(grad_send.at[k, q], grad_recv.at[k, x], *sems, (mine, 4 * y + q))

    def owned_grad(k):
        settle(grad_recv.at[k], last_recv.at[2 + k])
        total = grad_recv[k, 0].astype(jnp.float32)
        for i in range(1, XS):
            total = total + grad_recv[k, i].astype(jnp.float32)
        return total

    for t in range(TICKS):
        forward_first(t)
        if t > 0:
            backward_third(t - 1)
        forward_latent = forward_second(t)
        if t > 0:
            grad_down(t - 1)
            stash_first(t)
        forward_third(t)
        if t == 0:
            stash_first(t)
        if t < TICKS - 1:
            spread_stash(t + 1)
        backward_first(t)
        stash_latent = stash_second(t)
        backward_second(t, forward_latent, stash_latent)
        grad_up(t)
    to_owners(1)
    backward_third(TICKS - 1)
    grad_down(TICKS - 1)
    to_owners(0)

    up_ref[...] = owned_grad(1).T
    settle(out_ref, last_recv.at[0])

    for k in (DOWN, UP):
        settle_sent(grad_send.at[0], 4, spread_send.at[k])
    for k in (CARRIED, PENDING, *range(STASH, STASH + TICKS)):
        settle_sent(x_now, PEERS, spread_send.at[k])

    @pl.when(jnp.logical_not(gain_home))
    def _():
        settle(gain_row, spread_send.at[GAIN])

    @pl.when(z == 0)
    def _():
        @pl.when(core == 0)
        def _():
            settle(fresh_all.at[:, pl.ds(0, 2 * YS - 1)], spread_send.at[FRESH])

        @pl.when(core == 1)
        def _():
            settle(fresh_all.at[:, pl.ds(0, 2 * YS)], spread_send.at[FRESH])

    for t in range(TICKS):
        for kind, ref in enumerate((f_recv, s_recv, b_recv)):
            settle(ref.at[t], sum_send.at[kind, t])
        for kind, ref in enumerate((f_rows, s_rows, b_rows)):
            settle(ref.at[t, pl.ds(0, YS - 1)], sum_send.at[F_ROWS + kind, t])
        if t < TICKS - 1:
            settle(x_out.at[t], hop_send.at[0, t])
            settle(v_out.at[t], hop_send.at[1, t])
    settle_sent(x_now, PEERS, last_send.at[0])
    settle_sent(grad_send.at[1], 4, last_send.at[3])
    down_ref[...] = owned_grad(0)
    settle(ret_ref, last_recv.at[1])
    settle_sent(x_now, PEERS, last_send.at[1])
    settle_sent(grad_send.at[0], 4, last_send.at[2])


def shards(
    planes,
    carried,
    pending,
    stashed_inputs,
    fresh_batches,
    cotangent,
    norm_gain,
    w_down,
    w_up,
    forward_route,
    backward_route,
):
    row_count, width = carried.shape[2:]
    shard, rank = w_down.shape[1:]
    tokens, columns = row_count // XS, width // YS
    rows = PEERS * tokens
    share = rows // YS

    block = (PEERS, tokens, columns)
    bf16, f32 = jnp.bfloat16, jnp.float32
    dma = pltpu.SemaphoreType.DMA
    any_space = pl.BlockSpec(memory_space=pl.ANY)
    in_vmem = pl.BlockSpec(memory_space=pltpu.VMEM)
    in_smem = pl.BlockSpec(memory_space=pltpu.SMEM)
    outgoing, returning, grad_down, grad_up = pl.pallas_call(
        functools.partial(kernel, planes, width),
        out_shape=(
            jax.ShapeDtypeStruct((row_count, width), bf16),
            jax.ShapeDtypeStruct((row_count, width), bf16),
            jax.ShapeDtypeStruct((shard, rank), f32),
            jax.ShapeDtypeStruct((rank, shard), f32),
        ),
        in_specs=[in_smem] * 2 + [any_space] * 8,
        out_specs=(any_space, any_space, in_vmem, in_vmem),
        scratch_shapes=[
            pltpu.SMEM((2 * (TICKS - 1), PEERS), jnp.int32),
            pltpu.VMEM((1, columns), f32),
            pltpu.VMEM((rank, shard), bf16),
            pltpu.VMEM((shard, rank), bf16),
            pltpu.VMEM(block, bf16),
            pltpu.VMEM(block, bf16),
            pltpu.VMEM((rows, columns), bf16),
            pltpu.VMEM((TICKS, *block), bf16),
            pltpu.VMEM((TICKS - 1, *block), bf16),
            (pltpu.VMEM(block, bf16),) * (TICKS - 1),
            (pltpu.VMEM(block, bf16),) * (TICKS - 1),
            pltpu.VMEM((TICKS, *block), bf16),
            pltpu.VMEM((TICKS, *block), bf16),
            pltpu.VMEM((TICKS, YS, share + SPARE, rank), bf16),
            pltpu.VMEM((TICKS, YS - 1, share + SPARE, rank), bf16),
            pltpu.VMEM((TICKS, YS, share + SPARE, rank), bf16),
            pltpu.VMEM((TICKS, YS - 1, share + SPARE, rank), bf16),
            pltpu.VMEM((TICKS, YS, share, rank), bf16),
            pltpu.VMEM((TICKS, YS - 1, share, rank), bf16),
            pltpu.VMEM((TICKS, YS, share, rank), bf16),
            pltpu.VMEM((TICKS, YS, share, rank), bf16),
            pltpu.VMEM((TICKS, YS, share + SPARE, rank), bf16),
            pltpu.VMEM((columns, rank), bf16),
            pltpu.VMEM((columns, rank), bf16),
            pltpu.VMEM((2, columns, rank), f32),
            pltpu.VMEM((2, 4, shard, rank), bf16),
            pltpu.VMEM((2, XS, shard, rank), bf16),
            dma(()),
            dma((STASH + TICKS,)),
            dma((STASH + TICKS,)),
            dma((6, TICKS)),
            dma((6, TICKS)),
            dma((2, TICKS - 1)),
            dma((2, TICKS - 1)),
            dma((4,)),
            dma((4,)),
        ],
        compiler_params=pltpu.CompilerParams(
            collective_id=0, has_side_effects=True, vmem_limit_bytes=52 * 1024 * 1024
        ),
    )(
        forward_route,
        backward_route,
        carried[0, 0],
        pending[0, 0],
        stashed_inputs[0, 0],
        fresh_batches[:, 0],
        cotangent[:, 0],
        norm_gain,
        w_down[0],
        w_up[0],
    )
    return outgoing[None, None], returning[None, None], grad_down[None], grad_up[None]


def solution(mesh):
    planes = mesh.shape["section"] // 2
    in_specs = (
        P("section", "peer", None, None),
        P("section", "peer", None, None),
        P("section", "peer", None, None, None),
        P(None, "peer", None, None),
        P(None, "peer", None, None),
        P("section", None),
        P("section", "peer", None),
        P("section", None, "peer"),
        P(),
        P(),
    )
    out_specs = (
        P("section", "peer", None, None),
        P("section", "peer", None, None),
        P("section", "peer", None),
        P("section", None, "peer"),
    )
    return jax.shard_map(
        functools.partial(shards, planes), mesh=mesh, in_specs=in_specs, out_specs=out_specs, check_vma=False
    )
```

```python
import functools

import jax
import jax.numpy as jnp
from jax import lax
from jax.experimental import pallas as pl
from jax.experimental.pallas import tpu as pltpu
from jax.sharding import PartitionSpec as P

MESH = pl.DeviceIdType.MESH
NORM_EPS = 1e-05
TICKS = 4
XS = 4
YS = 4
PEERS = 16
LANES = 128
STEP = 256
SPARE = 16

DOWN, CARRIED, UP, PENDING, FRESH, GAIN, STASH = 0, 1, 2, 3, 4, 5, 6
F_SUM, S_SUM, B_SUM, F_ROWS, S_ROWS, B_ROWS = range(6)


def iota(shape, dim):
    return lax.broadcasted_iota(jnp.int32, shape, dim)


def to_row(column, first, length):
    shape = (column.shape[0], length)
    return jnp.sum(jnp.where(iota(shape, 1) == iota(shape, 0) + first, column, 0.0), axis=0, keepdims=True)


def to_column(row, first, count):
    shape = (count, row.shape[1])
    return jnp.sum(jnp.where(iota(shape, 1) == iota(shape, 0) + first, row, 0.0), axis=1, keepdims=True)


def in_two(row):
    high = row.astype(jnp.bfloat16).astype(jnp.float32)
    shape = (SPARE, row.shape[1])
    sub = iota(shape, 0)
    return jnp.where(sub == 0, high, jnp.where(sub == 1, row - high, 0.0)).astype(jnp.bfloat16)


def product(a, b, left, right):
    return lax.dot_general(a, b, (((left,), (right,)), ((), ())), preferred_element_type=jnp.float32)


def kernel(
    planes,
    width,
    forward_route,
    backward_route,
    carried,
    pending,
    stash,
    fresh,
    cotangent,
    gain,
    w_down,
    w_up,
    out_ref,
    ret_ref,
    down_ref,
    up_ref,
    inverse,
    gain_row,
    forward_here,
    backward_here,
    x_now,
    v_now,
    u_gained,
    u_all,
    fresh_all,
    x_in,
    v_in,
    x_out,
    v_out,
    f_send,
    f_recv,
    s_send,
    s_recv,
    b_send,
    b_recv,
    f_rows,
    s_rows,
    b_rows,
    down_all,
    up_all,
    grad_sum,
    grad_send,
    grad_recv,
    local_sem,
    spread_send,
    spread_recv,
    sum_send,
    sum_recv,
    hop_send,
    hop_recv,
    last_send,
    last_recv,
):
    section = lax.axis_index("section")
    peer = lax.axis_index("peer")
    z, x_hi = section // 2, section % 2
    y, x_lo, core = peer // 4, (peer // 2) % 2, peer % 2
    x = 2 * x_hi + x_lo
    mine = 2 * z + core
    tokens, columns = x_now.shape[1], x_now.shape[2]
    shard, rank = w_down.shape
    rows = PEERS * tokens
    share = rows // YS
    home = core == x_hi
    away = core != x_hi
    is_first = mine == 0
    is_last = mine == 2 * planes - 1
    sends_last = section == 2 * planes - 1

    def place(zz, xx, yy, cc):
        return (2 * zz + xx // 2, 4 * yy + 2 * (xx % 2) + cc)

    def remote(src, dst, send_sem, recv_sem, device):
        pltpu.make_async_remote_copy(
            src_ref=src,
            dst_ref=dst,
            send_sem=send_sem,
            recv_sem=recv_sem,
            device_id=device,
            device_id_type=MESH,
        ).start()

    def settle(ref, sem):
        pltpu.make_async_copy(ref, ref, sem).wait()

    route_copies = [
        pltpu.make_async_copy(route, there, local_sem.at[k])
        for k, (route, there) in enumerate(((forward_route, forward_here), (backward_route, backward_here)))
    ]
    for copy in route_copies:
        copy.start()

    barrier = pltpu.get_barrier_semaphore()
    z_up, z_down = (z + 1) % planes, (z + planes - 1) % planes

    @pl.loop(1, 32)
    def _(i):
        other = (x * 8 + y * 2 + core + i) % 32
        pl.semaphore_signal(
            barrier, inc=1, device_id=place(z, other // 8, (other // 2) % 4, other % 2), device_id_type=MESH
        )

    for zz in (z_up, z_down):
        pl.semaphore_signal(barrier, inc=1, device_id=place(zz, x, y, 1 - core), device_id_type=MESH)

    @pl.when(is_first)
    def _():
        @pl.loop(1, planes)
        def _(i):
            for cc in range(2):
                pl.semaphore_signal(
                    barrier,
                    inc=1,
                    device_id=place(i, 2 * x_hi + (x_lo + i // YS) % 2, (y + 2 * YS - i) % YS, cc),
                    device_id_type=MESH,
                )

    pl.semaphore_wait(barrier, jnp.where(z == 0, 33, 34))

    def cut_of(ref, xx, yy):
        tok = pl.ds(pl.multiple_of(xx * tokens, tokens), tokens)
        col = pl.ds(pl.multiple_of(yy * columns, LANES), columns)
        return ref.at[tok, col] if len(ref.shape) == 2 else ref.at[:, tok, col]

    def spread(source, target, k):
        sems = (spread_send.at[k], spread_recv.at[k])

        @pl.when(home)
        def _():
            pltpu.make_async_copy(cut_of(source, x, y), target.at[peer], sems[1]).start()

        @pl.when(away)
        def _():
            remote(cut_of(source, x, y), target.at[peer], *sems, place(z, x, y, x_hi))

        @pl.loop(1, XS * YS)
        def _(i):
            xx, yy = (x + i // YS) % XS, (y + i) % YS
            remote(cut_of(source, xx, yy), target.at[peer], *sems, place(z, xx, yy, x_hi))

    def spread_weight(source, target, k):
        sems = (spread_send.at[k], spread_recv.at[k])
        block = target.at[pl.ds(pl.multiple_of((2 * x_lo + core) * shard, 16), shard)]

        @pl.when(home)
        def _():
            pltpu.make_async_copy(source, block, sems[1]).start()

        @pl.when(away)
        def _():
            remote(source, block, *sems, place(z, x, y, x_hi))

        @pl.loop(1, XS)
        def _(i):
            remote(source, block, *sems, place(z, (x + i) % XS, y, x_hi))

    def settle_sent(ref, count, sem):
        @pl.when(home)
        def _():
            settle(ref.at[pl.ds(0, count - 1)], sem)

        @pl.when(away)
        def _():
            settle(ref.at[pl.ds(0, count)], sem)

    def spread_stash(t):
        @pl.when(sends_last)
        def _():
            spread(cotangent.at[t], u_all.at[t], STASH + t)

        @pl.when(jnp.logical_not(sends_last))
        def _():
            spread(stash.at[t], u_all.at[t], STASH + t)

    gain_home = jnp.logical_and(home, x == 2 * x_lo + core)
    gain_cut = gain.at[:, pl.ds(pl.multiple_of(y * columns, LANES), columns)]

    @pl.when(gain_home)
    def _():
        pltpu.make_async_copy(gain_cut, gain_row, spread_recv.at[GAIN]).start()

    @pl.when(jnp.logical_not(gain_home))
    def _():
        remote(
            gain_cut, gain_row, spread_send.at[GAIN], spread_recv.at[GAIN], place(z, 2 * x_lo + core, y, x_hi)
        )

    spread_weight(w_down, down_all, DOWN)
    spread(carried, x_now, CARRIED)
    spread_weight(w_up, up_all, UP)
    spread_stash(0)
    spread(pending, v_now, PENDING)

    fresh_x, fresh_y = 2 * x_hi + (x_lo + z // YS) % 2, (y + z) % YS
    fresh_home = jnp.logical_and(z == 0, core == 0)

    @pl.when(fresh_home)
    def _():
        pltpu.make_async_copy(cut_of(fresh, x, y), fresh_all.at[:, peer], spread_recv.at[FRESH]).start()

    @pl.when(jnp.logical_not(fresh_home))
    def _():
        remote(
            cut_of(fresh, fresh_x, fresh_y),
            fresh_all.at[:, peer],
            spread_send.at[FRESH],
            spread_recv.at[FRESH],
            place(0, fresh_x, fresh_y, 0),
        )

    grad_sum[...] = jnp.zeros_like(grad_sum)

    for copy in route_copies:
        copy.wait()
    boundary = (jnp.maximum(mine - 1, 0), jnp.minimum(mine, 2 * planes - 2))
    for t in range(TICKS - 1):
        for way, route in enumerate((forward_here, backward_here)):
            goes_to = [route[t, boundary[way], q] for q in range(PEERS)]

            @pl.loop(0, PEERS)
            def _(p):
                comes_from = 0
                for q in range(1, PEERS):
                    comes_from = jnp.where(goes_to[q] == p, q, comes_from)
                inverse[way * (TICKS - 1) + t, p] = comes_from

    def flat(value):
        return value.reshape(rows, value.shape[-1])

    def times_gain(value):
        return (value.astype(jnp.float32) * gain_row[...]).astype(jnp.bfloat16)

    def squares_row(value):
        value = value.astype(jnp.float32)
        return in_two(to_row(jnp.sum(value * value, axis=-1, keepdims=True), 0, rows))

    def send_sums(source, target, kind, t):
        for i in range(1, YS):
            yy = (y + i) % YS
            remote(
                source.at[t, yy],
                target.at[t, i - 1],
                sum_send.at[kind, t],
                sum_recv.at[kind, t],
                place(z, x, yy, core),
            )

    def take_sum(source, target, kind, t):
        settle(target.at[t], sum_recv.at[kind, t])
        total = source[t, y].astype(jnp.float32)
        for i in range(YS - 1):
            total = total + target[t, i].astype(jnp.float32)
        return total

    def send_rows(target, kind, t):
        for i in range(1, YS):
            remote(
                target.at[t, y],
                target.at[t, y],
                sum_send.at[kind, t],
                sum_recv.at[kind, t],
                place(z, x, (y + i) % YS, core),
            )

    def take_rows(target, kind, t):
        settle(target.at[t, pl.ds(0, YS - 1)], sum_recv.at[kind, t])

    def scale_of(total):
        squares = to_column(total[share : share + 1] + total[share + 1 : share + 2], y * share, share)
        return lax.rsqrt(squares * (1.0 / width) + NORM_EPS)

    def put_sums(target, t, value):
        target[t, :, 0:share, :] = value.astype(jnp.bfloat16).reshape(YS, share, rank)

    def put_squares(target, t, block):
        for yy in range(YS):
            target[t, yy, share:, :] = block

    def forward_first(t):
        if t == 0:
            settle(down_all, spread_recv.at[DOWN])
            settle(gain_row, spread_recv.at[GAIN])
            settle(x_now, spread_recv.at[CARRIED])
        else:
            settle(x_in[t - 1], hop_recv.at[0, t - 1])

            @pl.when(is_first)
            def _():
                if t == 1:
                    settle(fresh_all, spread_recv.at[FRESH])
                x_now[...] = fresh_all[t - 1]

            @pl.when(jnp.logical_not(is_first))
            def _():
                for p in range(PEERS):
                    x_now[p] = x_in[t - 1][inverse[t - 1, p]]

        x_rows = flat(x_now[...])
        put_sums(f_send, t, product(times_gain(x_rows), down_all[...], 1, 0))
        put_squares(f_send, t, squares_row(x_rows))
        send_sums(f_send, f_recv, F_SUM, t)

    def forward_second(t):
        total = take_sum(f_send, f_recv, F_SUM, t)
        scale = scale_of(total)
        latent = total[0:share] * scale
        f_rows[t, y] = (latent * jax.nn.sigmoid(latent)).astype(jnp.bfloat16)
        send_rows(f_rows, F_ROWS, t)
        return latent, scale

    def forward_third(t):
        if t == 0:
            settle(up_all, spread_recv.at[UP])
        take_rows(f_rows, F_ROWS, t)
        hidden = flat(f_rows[t])
        for start in range(0, columns, STEP):
            cut = slice(start, start + STEP)
            result = flat(x_now[:, :, cut]).astype(jnp.float32) + product(hidden, up_all[cut, :], 1, 1)
            x_out[t, :, :, cut] = result.astype(jnp.bfloat16).reshape(PEERS, tokens, STEP)
            if t < TICKS - 1:
                remote(
                    x_out.at[t, :, :, cut],
                    x_in[t].at[:, :, cut],
                    hop_send.at[0, t],
                    hop_recv.at[0, t],
                    place((z + core) % planes, x, y, 1 - core),
                )
        if t == TICKS - 1:
            to_peers(x_out.at[t], out_ref, 0)

    def stash_first(t):
        settle(u_all.at[t], spread_recv.at[STASH + t])
        u_rows = flat(u_all[t])
        u_gained[...] = times_gain(u_rows)
        put_sums(s_send, t, product(u_gained[...], down_all[...], 1, 0))
        put_squares(s_send, t, squares_row(u_rows))
        send_sums(s_send, s_recv, S_SUM, t)

    def stash_second(t):
        total = take_sum(s_send, s_recv, S_SUM, t)
        scale = scale_of(total)
        latent = total[0:share] * scale
        s_rows[t, y] = (latent * jax.nn.sigmoid(latent)).astype(jnp.bfloat16)
        send_rows(s_rows, S_ROWS, t)
        return latent, scale

    def backward_first(t):
        if t == 0:
            settle(v_now, spread_recv.at[PENDING])
        else:
            settle(v_in[t - 1], hop_recv.at[1, t - 1])
            for p in range(PEERS):
                v_now[p] = v_in[t - 1][inverse[TICKS - 2 + t, p]]

        @pl.when(is_last)
        def _():
            v_now[...] = u_all[t]
            u_all[t] = x_now[...]
            u_gained[...] = times_gain(flat(x_now[...]))

        put_sums(b_send, t, product(flat(v_now[...]), up_all[...], 1, 0))
        send_sums(b_send, b_recv, B_SUM, t)

    def backward_second(t, forward_latent, stash_latent):
        total = take_sum(b_send, b_recv, B_SUM, t)
        latent = jnp.where(is_last, forward_latent[0], stash_latent[0])
        scale = jnp.where(is_last, forward_latent[1], stash_latent[1])
        sigmoid = jax.nn.sigmoid(latent)
        latent_grad = total * sigmoid * (1.0 + latent * (1.0 - sigmoid))
        b_rows[t, y, 0:share, :] = (latent_grad * scale).astype(jnp.bfloat16)
        along = jnp.sum(latent_grad * latent, axis=-1, keepdims=True) * (scale * scale * (1.0 / width))
        b_rows[t, y, share:, :] = in_two(to_row(along, y * share, rows))
        send_rows(b_rows, B_ROWS, t)

    def backward_third(t):
        take_rows(b_rows, B_ROWS, t)
        latent_grad = flat(b_rows[t, :, 0:share, :])
        extra = b_rows[t, :, share:, :].astype(jnp.float32)
        along = to_column(jnp.sum(extra[:, 0:1] + extra[:, 1:2], axis=0), 0, rows)
        for start in range(0, columns, STEP):
            cut = slice(start, start + STEP)
            result = (
                flat(v_now[:, :, cut]).astype(jnp.float32)
                + product(latent_grad, down_all[cut, :], 1, 1) * gain_row[:, cut]
                - flat(u_all[t, :, :, cut]).astype(jnp.float32) * along
            )
            v_out[t, :, :, cut] = result.astype(jnp.bfloat16).reshape(PEERS, tokens, STEP)
            if t < TICKS - 1:
                remote(
                    v_out.at[t, :, :, cut],
                    v_in[t].at[:, :, cut],
                    hop_send.at[1, t],
                    hop_recv.at[1, t],
                    place((z + core + planes - 1) % planes, x, y, 1 - core),
                )
        if t == TICKS - 1:
            to_peers(v_out.at[t], ret_ref, 1)

    def to_peers(source, target, k):
        sems = (last_send.at[k], last_recv.at[k])
        block = cut_of(target, x, y)

        @pl.when(home)
        def _():
            pltpu.make_async_copy(source.at[peer], block, sems[1]).start()

        @pl.when(away)
        def _():
            remote(source.at[peer], block, *sems, (mine, peer))

        @pl.loop(1, PEERS)
        def _(i):
            q = (peer + i) % PEERS
            remote(source.at[q], block, *sems, (mine, q))

    def grad_up(t, may_be_last):
        take_rows(s_rows, S_ROWS, t)
        hidden = flat(s_rows[t])
        if may_be_last:
            hidden = jnp.where(is_last, flat(f_rows[t]), hidden)
        for start in range(0, columns, STEP):
            cut = slice(start, start + STEP)
            grad_sum[1, cut, :] += product(flat(v_now[:, :, cut]), hidden, 0, 0)

    def grad_down(t):
        latent_grad = flat(b_rows[t, :, 0:share, :])
        for start in range(0, columns, STEP):
            cut = slice(start, start + STEP)
            grad_sum[0, cut, :] += product(u_gained[:, cut], latent_grad, 0, 0)

    def to_owners(k):
        for q in range(4):
            grad_send[k, q] = grad_sum[k, q * shard : (q + 1) * shard, :].astype(jnp.bfloat16)
        sems = (last_send.at[2 + k], last_recv.at[2 + k])
        own = 2 * x_lo + core

        @pl.when(home)
        def _():
            pltpu.make_async_copy(grad_send.at[k, own], grad_recv.at[k, x], sems[1]).start()

        @pl.when(away)
        def _():
            remote(grad_send.at[k, own], grad_recv.at[k, x], *sems, (mine, peer))

        @pl.loop(1, 4)
        def _(i):
            q = (own + i) % 4
            remote(grad_send.at[k, q], grad_recv.at[k, x], *sems, (mine, 4 * y + q))

    def owned_grad(k):
        settle(grad_recv.at[k], last_recv.at[2 + k])
        total = grad_recv[k, 0].astype(jnp.float32)
        for i in range(1, XS):
            total = total + grad_recv[k, i].astype(jnp.float32)
        return total

    forward_first(0)
    latent = forward_second(0)
    forward_third(0)
    spread_stash(1)
    stash_first(0)
    backward_first(0)
    backward_second(0, latent, stash_second(0))
    grad_up(0, True)
    backward_third(0)
    grad_down(0)

    @pl.when(core == 0)
    def _():
        for t in range(1, TICKS):
            stash_first(t)
            if t < TICKS - 1:
                spread_stash(t + 1)
            backward_first(t)
            latent = stash_second(t)
            backward_second(t, latent, latent)
            forward_first(t)
            grad_up(t, False)
            if t == TICKS - 1:
                to_owners(1)
            backward_third(t)
            forward_second(t)
            grad_down(t)
            if t == TICKS - 1:
                to_owners(0)
            forward_third(t)

    @pl.when(core == 1)
    def _():
        for t in range(1, TICKS):
            stash_first(t)
            if t < TICKS - 1:
                spread_stash(t + 1)
            forward_first(t)
            backward_first(t)
            stash_latent = stash_second(t)
            latent = forward_second(t)
            backward_second(t, latent, stash_latent)
            forward_third(t)
            grad_up(t, True)
            if t == TICKS - 1:
                to_owners(1)
            backward_third(t)
            grad_down(t)
            if t == TICKS - 1:
                to_owners(0)

    up_ref[...] = owned_grad(1)
    settle(out_ref, last_recv.at[0])

    for k in (DOWN, UP):
        settle_sent(grad_send.at[0], 4, spread_send.at[k])
    for k in (CARRIED, PENDING, *range(STASH, STASH + TICKS)):
        settle_sent(x_now, PEERS, spread_send.at[k])

    @pl.when(jnp.logical_not(gain_home))
    def _():
        settle(gain_row, spread_send.at[GAIN])

    @pl.when(jnp.logical_not(fresh_home))
    def _():
        settle(fresh_all.at[:, 0], spread_send.at[FRESH])

    for t in range(TICKS):
        for kind, ref in enumerate((f_recv, s_recv, b_recv)):
            settle(ref.at[t], sum_send.at[kind, t])
        for kind, ref in enumerate((f_rows, s_rows, b_rows)):
            settle(ref.at[t, pl.ds(0, YS - 1)], sum_send.at[F_ROWS + kind, t])
        if t < TICKS - 1:
            settle(x_out.at[t], hop_send.at[0, t])
            settle(v_out.at[t], hop_send.at[1, t])
    settle_sent(x_now, PEERS, last_send.at[0])
    settle_sent(grad_send.at[1], 4, last_send.at[3])
    down_ref[...] = owned_grad(0)
    settle(ret_ref, last_recv.at[1])
    settle_sent(x_now, PEERS, last_send.at[1])
    settle_sent(grad_send.at[0], 4, last_send.at[2])


def shards(
    planes,
    carried,
    pending,
    stashed_inputs,
    fresh_batches,
    cotangent,
    norm_gain,
    w_down,
    w_up,
    forward_route,
    backward_route,
):
    row_count, width = carried.shape[2:]
    shard, rank = w_down.shape[1:]
    tokens, columns = row_count // XS, width // YS
    rows = PEERS * tokens
    share = rows // YS
    assert planes == 2 * YS

    block = (PEERS, tokens, columns)
    bf16, f32 = jnp.bfloat16, jnp.float32
    dma = pltpu.SemaphoreType.DMA
    in_hbm = pl.BlockSpec(memory_space=pltpu.HBM)
    in_vmem = pl.BlockSpec(memory_space=pltpu.VMEM)
    outgoing, returning, grad_down, grad_up = pl.pallas_call(
        functools.partial(kernel, planes, width),
        out_shape=(
            jax.ShapeDtypeStruct((row_count, width), bf16),
            jax.ShapeDtypeStruct((row_count, width), bf16),
            jax.ShapeDtypeStruct((shard, rank), f32),
            jax.ShapeDtypeStruct((shard, rank), f32),
        ),
        in_specs=[in_hbm] * 10,
        out_specs=(in_hbm, in_hbm, in_vmem, in_vmem),
        scratch_shapes=[
            pltpu.SMEM((2 * (TICKS - 1), PEERS), jnp.int32),
            pltpu.VMEM((1, columns), f32),
            pltpu.SMEM(forward_route.shape, jnp.int32),
            pltpu.SMEM(backward_route.shape, jnp.int32),
            pltpu.VMEM(block, bf16),
            pltpu.VMEM(block, bf16),
            pltpu.VMEM((rows, columns), bf16),
            pltpu.VMEM((TICKS, *block), bf16),
            pltpu.VMEM((TICKS - 1, *block), bf16),
            (pltpu.VMEM(block, bf16),) * (TICKS - 1),
            (pltpu.VMEM(block, bf16),) * (TICKS - 1),
            pltpu.VMEM((TICKS, *block), bf16),
            pltpu.VMEM((TICKS, *block), bf16),
            pltpu.VMEM((TICKS, YS, share + SPARE, rank), bf16),
            pltpu.VMEM((TICKS, YS - 1, share + SPARE, rank), bf16),
            pltpu.VMEM((TICKS, YS, share + SPARE, rank), bf16),
            pltpu.VMEM((TICKS, YS - 1, share + SPARE, rank), bf16),
            pltpu.VMEM((TICKS, YS, share, rank), bf16),
            pltpu.VMEM((TICKS, YS - 1, share, rank), bf16),
            pltpu.VMEM((TICKS, YS, share, rank), bf16),
            pltpu.VMEM((TICKS, YS, share, rank), bf16),
            pltpu.VMEM((TICKS, YS, share + SPARE, rank), bf16),
            pltpu.VMEM((columns, rank), bf16),
            pltpu.VMEM((columns, rank), bf16),
            pltpu.VMEM((2, columns, rank), f32),
            pltpu.VMEM((2, 4, shard, rank), bf16),
            pltpu.VMEM((2, XS, shard, rank), bf16),
            dma((2,)),
            dma((STASH + TICKS,)),
            dma((STASH + TICKS,)),
            dma((6, TICKS)),
            dma((6, TICKS)),
            dma((2, TICKS - 1)),
            dma((2, TICKS - 1)),
            dma((4,)),
            dma((4,)),
        ],
        compiler_params=pltpu.CompilerParams(
            collective_id=0, has_side_effects=True, vmem_limit_bytes=56 * 1024 * 1024
        ),
    )(
        forward_route,
        backward_route,
        carried[0, 0],
        pending[0, 0],
        stashed_inputs[0, 0],
        fresh_batches[:, 0],
        cotangent[:, 0],
        norm_gain,
        w_down[0],
        w_up[0].T,
    )
    return outgoing[None, None], returning[None, None], grad_down[None], grad_up.T[None]


def solution(mesh):
    planes = mesh.shape["section"] // 2
    in_specs = (
        P("section", "peer", None, None),
        P("section", "peer", None, None),
        P("section", "peer", None, None, None),
        P(None, "peer", None, None),
        P(None, "peer", None, None),
        P("section", None),
        P("section", "peer", None),
        P("section", None, "peer"),
        P(),
        P(),
    )
    out_specs = (
        P("section", "peer", None, None),
        P("section", "peer", None, None),
        P("section", "peer", None),
        P("section", None, "peer"),
    )
    return jax.shard_map(
        functools.partial(shards, planes), mesh=mesh, in_specs=in_specs, out_specs=out_specs, check_vma=False
    )
```

```python
import functools

import jax
import jax.numpy as jnp
from jax import lax
from jax.experimental import pallas as pl
from jax.experimental.pallas import tpu as pltpu
from jax.sharding import PartitionSpec as P

MESH = pl.DeviceIdType.MESH
NORM_EPS = 1e-05
TICKS = 4
XS = 4
YS = 4
PEERS = 16
LANES = 128
STEP = 256
SPARE = 16

DOWN, CARRIED, UP, PENDING, GAIN, FRESH, RELAY, STASH = 0, 1, 2, 3, 4, 5, 8, 11
F_SUM, S_SUM, B_SUM, F_ROWS, S_ROWS, B_ROWS = range(6)


def iota(shape, dim):
    return lax.broadcasted_iota(jnp.int32, shape, dim)


def to_row(column, first, length):
    shape = (column.shape[0], length)
    return jnp.sum(jnp.where(iota(shape, 1) == iota(shape, 0) + first, column, 0.0), axis=0, keepdims=True)


def to_column(row, first, count):
    shape = (count, row.shape[1])
    return jnp.sum(jnp.where(iota(shape, 1) == iota(shape, 0) + first, row, 0.0), axis=1, keepdims=True)


def in_two(row):
    high = row.astype(jnp.bfloat16).astype(jnp.float32)
    shape = (SPARE, row.shape[1])
    sub = iota(shape, 0)
    return jnp.where(sub == 0, high, jnp.where(sub == 1, row - high, 0.0)).astype(jnp.bfloat16)


def product(a, b, left, right):
    return lax.dot_general(a, b, (((left,), (right,)), ((), ())), preferred_element_type=jnp.float32)


def kernel(
    planes,
    width,
    forward_route,
    backward_route,
    carried,
    pending,
    stash,
    fresh,
    cotangent,
    gain,
    w_down,
    w_up,
    out_ref,
    ret_ref,
    down_ref,
    up_ref,
    inverse,
    gain_row,
    forward_here,
    backward_here,
    x_now,
    v_now,
    u_gained,
    u_all,
    fresh_all,
    relay,
    x_in,
    v_in,
    x_out,
    v_out,
    f_send,
    f_recv,
    s_send,
    s_recv,
    b_send,
    b_recv,
    f_rows,
    s_rows,
    b_rows,
    down_all,
    up_all,
    grad_sum,
    grad_send,
    grad_recv,
    local_sem,
    spread_send,
    spread_recv,
    sum_send,
    sum_recv,
    hop_send,
    hop_recv,
    last_send,
    last_recv,
):
    section = lax.axis_index("section")
    peer = lax.axis_index("peer")
    z, x_hi = section // 2, section % 2
    y, x_lo, core = peer // 4, (peer // 2) % 2, peer % 2
    x = 2 * x_hi + x_lo
    mine = 2 * z + core
    tokens, columns = x_now.shape[1], x_now.shape[2]
    shard, rank = w_down.shape
    rows = PEERS * tokens
    share = rows // YS
    home = core == x_hi
    away = core != x_hi
    is_first = mine == 0
    is_last = mine == 2 * planes - 1
    sends_last = section == 2 * planes - 1

    def place(zz, xx, yy, cc):
        return (2 * zz + xx // 2, 4 * yy + 2 * (xx % 2) + cc)

    def remote(src, dst, send_sem, recv_sem, device):
        pltpu.make_async_remote_copy(
            src_ref=src,
            dst_ref=dst,
            send_sem=send_sem,
            recv_sem=recv_sem,
            device_id=device,
            device_id_type=MESH,
        ).start()

    def settle(ref, sem):
        pltpu.make_async_copy(ref, ref, sem).wait()

    route_copies = [
        pltpu.make_async_copy(route, there, local_sem.at[k])
        for k, (route, there) in enumerate(((forward_route, forward_here), (backward_route, backward_here)))
    ]
    for copy in route_copies:
        copy.start()

    barrier = pltpu.get_barrier_semaphore()
    z_up, z_down = (z + 1) % planes, (z + planes - 1) % planes

    @pl.loop(1, 32)
    def _(i):
        other = (x * 8 + y * 2 + core + i) % 32
        pl.semaphore_signal(
            barrier, inc=1, device_id=place(z, other // 8, (other // 2) % 4, other % 2), device_id_type=MESH
        )

    for zz in (z_up, z_down):
        pl.semaphore_signal(barrier, inc=1, device_id=place(zz, x, y, 1 - core), device_id_type=MESH)


    @pl.when(is_first)
    def _():
        @pl.loop(1, planes)
        def _(i):
            for cc in range(2):
                pl.semaphore_signal(barrier, inc=1, device_id=place(i, x, y, cc), device_id_type=MESH)

    pl.semaphore_wait(barrier, jnp.where(z == 0, 33, 34))

    def cut_of(ref, xx, yy):
        tok = pl.ds(pl.multiple_of(xx * tokens, tokens), tokens)
        col = pl.ds(pl.multiple_of(yy * columns, LANES), columns)
        return ref.at[tok, col] if len(ref.shape) == 2 else ref.at[:, tok, col]

    def spread(source, target, k, first=0, count=XS * YS):
        sems = (spread_send.at[k], spread_recv.at[k])

        if first == 0:

            @pl.when(home)
            def _():
                pltpu.make_async_copy(cut_of(source, x, y), target.at[peer], sems[1]).start()

            @pl.when(away)
            def _():
                remote(cut_of(source, x, y), target.at[peer], *sems, place(z, x, y, x_hi))

        @pl.loop(max(first, 1), first + count)
        def _(i):
            xx, yy = (x + i // YS) % XS, (y + i) % YS
            remote(cut_of(source, xx, yy), target.at[peer], *sems, place(z, xx, yy, x_hi))

    def spread_weight(source, target, k):
        sems = (spread_send.at[k], spread_recv.at[k])
        block = target.at[pl.ds(pl.multiple_of((2 * x_lo + core) * shard, 16), shard)]

        @pl.when(home)
        def _():
            pltpu.make_async_copy(source, block, sems[1]).start()

        @pl.when(away)
        def _():
            remote(source, block, *sems, place(z, x, y, x_hi))

        @pl.loop(1, XS)
        def _(i):
            remote(source, block, *sems, place(z, (x + i) % XS, y, x_hi))

    def settle_sent(ref, count, sem):
        @pl.when(home)
        def _():
            settle(ref.at[pl.ds(0, count - 1)], sem)

        @pl.when(away)
        def _():
            settle(ref.at[pl.ds(0, count)], sem)

    def fresh_shift(t):
        shift = (z + (TICKS - 1) * t) % planes
        return shift // YS, shift % YS

    def relay_fresh(t):
        by_x, by_y = fresh_shift(t)
        xx, yy = 2 * x_hi + (x_lo + by_x) % 2, (y + by_y) % YS
        stays = by_x + by_y == 0

        @pl.when(stays)
        def _():
            pltpu.make_async_copy(cut_of(fresh.at[t], x, y), relay.at[t], spread_recv.at[RELAY + t]).start()

        @pl.when(jnp.logical_not(stays))
        def _():
            remote(
                cut_of(fresh.at[t], xx, yy),
                relay.at[t],
                spread_send.at[RELAY + t],
                spread_recv.at[RELAY + t],
                place(z, xx, yy, core),
            )

    def drop_fresh(t):
        by_x, by_y = fresh_shift(t)
        settle(relay.at[t], spread_recv.at[RELAY + t])
        target = fresh_all.at[t, 4 * ((y + YS - by_y) % YS) + 2 * ((x_lo + 2 - by_x) % 2) + core]

        @pl.when(is_first)
        def _():
            pltpu.make_async_copy(relay.at[t], target, spread_recv.at[FRESH + t]).start()

        @pl.when(jnp.logical_not(is_first))
        def _():
            remote(relay.at[t], target, spread_send.at[FRESH + t], spread_recv.at[FRESH + t], place(0, x, y, 0))

    def spread_stash(t, *parts):
        @pl.when(sends_last)
        def _():
            spread(cotangent.at[t], u_all.at[t], STASH + t, *parts)

        @pl.when(jnp.logical_not(sends_last))
        def _():
            spread(stash.at[t], u_all.at[t], STASH + t, *parts)

    def stash_part(t, part):
        if 0 < t < TICKS - 1:
            spread_stash(t + 1, 4 * part, 4)

    gain_home = jnp.logical_and(home, x == 2 * x_lo + core)
    gain_cut = gain.at[:, pl.ds(pl.multiple_of(y * columns, LANES), columns)]

    @pl.when(gain_home)
    def _():
        pltpu.make_async_copy(gain_cut, gain_row, spread_recv.at[GAIN]).start()

    @pl.when(jnp.logical_not(gain_home))
    def _():
        remote(
            gain_cut, gain_row, spread_send.at[GAIN], spread_recv.at[GAIN], place(z, 2 * x_lo + core, y, x_hi)
        )

    for t in range(TICKS - 1):
        relay_fresh(t)
    spread_weight(w_down, down_all, DOWN)
    spread(carried, x_now, CARRIED)
    spread_weight(w_up, up_all, UP)
    spread_stash(0)
    spread(pending, v_now, PENDING)
    for t in range(TICKS - 1):
        drop_fresh(t)

    grad_sum[...] = jnp.zeros_like(grad_sum)

    for copy in route_copies:
        copy.wait()
    boundary = (jnp.maximum(mine - 1, 0), jnp.minimum(mine, 2 * planes - 2))
    for t in range(TICKS - 1):
        for way, route in enumerate((forward_here, backward_here)):
            goes_to = [route[t, boundary[way], q] for q in range(PEERS)]

            @pl.loop(0, PEERS)
            def _(p):
                comes_from = 0
                for q in range(1, PEERS):
                    comes_from = jnp.where(goes_to[q] == p, q, comes_from)
                inverse[way * (TICKS - 1) + t, p] = comes_from

    def flat(value):
        return value.reshape(rows, value.shape[-1])

    def times_gain(value):
        return (value.astype(jnp.float32) * gain_row[...]).astype(jnp.bfloat16)

    def squares_row(value):
        value = value.astype(jnp.float32)
        return in_two(to_row(jnp.sum(value * value, axis=-1, keepdims=True), 0, rows))

    def send_sums(source, target, kind, t):
        for i in range(1, YS):
            yy = (y + i) % YS
            remote(
                source.at[t, yy],
                target.at[t, i - 1],
                sum_send.at[kind, t],
                sum_recv.at[kind, t],
                place(z, x, yy, core),
            )

    def take_sum(source, target, kind, t):
        settle(target.at[t], sum_recv.at[kind, t])
        total = source[t, y].astype(jnp.float32)
        for i in range(YS - 1):
            total = total + target[t, i].astype(jnp.float32)
        return total

    def send_rows(target, kind, t):
        for i in range(1, YS):
            remote(
                target.at[t, y],
                target.at[t, y],
                sum_send.at[kind, t],
                sum_recv.at[kind, t],
                place(z, x, (y + i) % YS, core),
            )

    def take_rows(target, kind, t):
        settle(target.at[t, pl.ds(0, YS - 1)], sum_recv.at[kind, t])

    def scale_of(total):
        squares = to_column(total[share : share + 1] + total[share + 1 : share + 2], y * share, share)
        return lax.rsqrt(squares * (1.0 / width) + NORM_EPS)

    def put_sums(target, t, value):
        target[t, :, 0:share, :] = value.astype(jnp.bfloat16).reshape(YS, share, rank)

    def put_squares(target, t, block):
        for yy in range(YS):
            target[t, yy, share:, :] = block

    def forward_first(t):
        if t == 0:
            settle(down_all, spread_recv.at[DOWN])
            settle(gain_row, spread_recv.at[GAIN])
            settle(x_now, spread_recv.at[CARRIED])
        else:
            settle(x_in[t - 1], hop_recv.at[0, t - 1])

            @pl.when(is_first)
            def _():
                settle(fresh_all.at[t - 1], spread_recv.at[FRESH + t - 1])
                x_now[...] = fresh_all[t - 1]

            @pl.when(jnp.logical_not(is_first))
            def _():
                for p in range(PEERS):
                    x_now[p] = x_in[t - 1][inverse[t - 1, p]]

        stash_part(t, 0)
        x_rows = flat(x_now[...])
        put_sums(f_send, t, product(times_gain(x_rows), down_all[...], 1, 0))
        put_squares(f_send, t, squares_row(x_rows))
        send_sums(f_send, f_recv, F_SUM, t)

    def forward_second(t):
        total = take_sum(f_send, f_recv, F_SUM, t)
        scale = scale_of(total)
        latent = total[0:share] * scale
        f_rows[t, y] = (latent * jax.nn.sigmoid(latent)).astype(jnp.bfloat16)
        send_rows(f_rows, F_ROWS, t)
        return latent, scale

    def forward_third(t):
        if t == 0:
            settle(up_all, spread_recv.at[UP])
        take_rows(f_rows, F_ROWS, t)
        stash_part(t, 2)
        hidden = flat(f_rows[t])
        for start in range(0, columns, STEP):
            cut = slice(start, start + STEP)
            result = flat(x_now[:, :, cut]).astype(jnp.float32) + product(hidden, up_all[cut, :], 1, 1)
            x_out[t, :, :, cut] = result.astype(jnp.bfloat16).reshape(PEERS, tokens, STEP)
            if t < TICKS - 1:
                remote(
                    x_out.at[t, :, :, cut],
                    x_in[t].at[:, :, cut],
                    hop_send.at[0, t],
                    hop_recv.at[0, t],
                    place((z + core) % planes, x, y, 1 - core),
                )
        if t == TICKS - 1:
            to_peers(x_out.at[t], out_ref, 0)

    def stash_first(t):
        settle(u_all.at[t], spread_recv.at[STASH + t])
        u_rows = flat(u_all[t])
        u_gained[...] = times_gain(u_rows)
        put_sums(s_send, t, product(u_gained[...], down_all[...], 1, 0))
        put_squares(s_send, t, squares_row(u_rows))
        send_sums(s_send, s_recv, S_SUM, t)

    def stash_second(t):
        total = take_sum(s_send, s_recv, S_SUM, t)
        scale = scale_of(total)
        latent = total[0:share] * scale
        s_rows[t, y] = (latent * jax.nn.sigmoid(latent)).astype(jnp.bfloat16)
        send_rows(s_rows, S_ROWS, t)
        return latent, scale

    def backward_first(t):
        if t == 0:
            settle(v_now, spread_recv.at[PENDING])
        else:
            settle(v_in[t - 1], hop_recv.at[1, t - 1])
            for p in range(PEERS):
                v_now[p] = v_in[t - 1][inverse[TICKS - 2 + t, p]]

        stash_part(t, 3)

        @pl.when(is_last)
        def _():
            v_now[...] = u_all[t]
            u_all[t] = x_now[...]
            u_gained[...] = times_gain(flat(x_now[...]))

        put_sums(b_send, t, product(flat(v_now[...]), up_all[...], 1, 0))
        send_sums(b_send, b_recv, B_SUM, t)

    def backward_second(t, forward_latent, stash_latent):
        total = take_sum(b_send, b_recv, B_SUM, t)
        latent = jnp.where(is_last, forward_latent[0], stash_latent[0])
        scale = jnp.where(is_last, forward_latent[1], stash_latent[1])
        sigmoid = jax.nn.sigmoid(latent)
        latent_grad = total * sigmoid * (1.0 + latent * (1.0 - sigmoid))
        b_rows[t, y, 0:share, :] = (latent_grad * scale).astype(jnp.bfloat16)
        along = jnp.sum(latent_grad * latent, axis=-1, keepdims=True) * (scale * scale * (1.0 / width))
        b_rows[t, y, share:, :] = in_two(to_row(along, y * share, rows))
        send_rows(b_rows, B_ROWS, t)

    def backward_third(t):
        take_rows(b_rows, B_ROWS, t)
        stash_part(t + 1, 1)
        latent_grad = flat(b_rows[t, :, 0:share, :])
        extra = b_rows[t, :, share:, :].astype(jnp.float32)
        along = to_column(jnp.sum(extra[:, 0:1] + extra[:, 1:2], axis=0), 0, rows)
        for start in range(0, columns, STEP):
            cut = slice(start, start + STEP)
            result = (
                flat(v_now[:, :, cut]).astype(jnp.float32)
                + product(latent_grad, down_all[cut, :], 1, 1) * gain_row[:, cut]
                - flat(u_all[t, :, :, cut]).astype(jnp.float32) * along
            )
            v_out[t, :, :, cut] = result.astype(jnp.bfloat16).reshape(PEERS, tokens, STEP)
            if t < TICKS - 1:
                remote(
                    v_out.at[t, :, :, cut],
                    v_in[t].at[:, :, cut],
                    hop_send.at[1, t],
                    hop_recv.at[1, t],
                    place((z + core + planes - 1) % planes, x, y, 1 - core),
                )
        if t == TICKS - 1:
            to_peers(v_out.at[t], ret_ref, 1)

    def to_peers(source, target, k):
        sems = (last_send.at[k], last_recv.at[k])
        block = cut_of(target, x, y)

        @pl.when(home)
        def _():
            pltpu.make_async_copy(source.at[peer], block, sems[1]).start()

        @pl.when(away)
        def _():
            remote(source.at[peer], block, *sems, (mine, peer))

        @pl.loop(1, PEERS)
        def _(i):
            q = (peer + i) % PEERS
            remote(source.at[q], block, *sems, (mine, q))

    def grad_up(t):
        take_rows(s_rows, S_ROWS, t)
        hidden = jnp.where(is_last, flat(f_rows[t]), flat(s_rows[t]))
        for start in range(0, columns, STEP):
            cut = slice(start, start + STEP)
            grad_sum[1, cut, :] += product(flat(v_now[:, :, cut]), hidden, 0, 0)

    def grad_down(t):
        latent_grad = flat(b_rows[t, :, 0:share, :])
        for start in range(0, columns, STEP):
            cut = slice(start, start + STEP)
            grad_sum[0, cut, :] += product(u_gained[:, cut], latent_grad, 0, 0)

    def to_owners(k):
        for q in range(4):
            grad_send[k, q] = grad_sum[k, q * shard : (q + 1) * shard, :].astype(jnp.bfloat16)
        sems = (last_send.at[2 + k], last_recv.at[2 + k])
        own = 2 * x_lo + core

        @pl.when(home)
        def _():
            pltpu.make_async_copy(grad_send.at[k, own], grad_recv.at[k, x], sems[1]).start()

        @pl.when(away)
        def _():
            remote(grad_send.at[k, own], grad_recv.at[k, x], *sems, (mine, peer))

        @pl.loop(1, 4)
        def _(i):
            q = (own + i) % 4
            remote(grad_send.at[k, q], grad_recv.at[k, x], *sems, (mine, 4 * y + q))

    def owned_grad(k):
        settle(grad_recv.at[k], last_recv.at[2 + k])
        total = grad_recv[k, 0].astype(jnp.float32)
        for i in range(1, XS):
            total = total + grad_recv[k, i].astype(jnp.float32)
        return total

    for t in range(TICKS):
        forward_first(t)
        if t > 0:
            backward_third(t - 1)
        latent = forward_second(t)
        if t > 0:
            grad_down(t - 1)
            stash_first(t)
        forward_third(t)
        if t == 0:
            spread_stash(1)
            stash_first(0)
        if t < TICKS - 1:
            backward_first(t)
            stash_latent = stash_second(t)
            backward_second(t, latent, stash_latent)
            grad_up(t)
        else:
            stash_latent = stash_second(t)
            backward_first(t)
            grad_up(t)
            to_owners(1)
            backward_second(t, latent, stash_latent)
    backward_third(TICKS - 1)
    grad_down(TICKS - 1)
    to_owners(0)

    up_ref[...] = owned_grad(1)
    settle(out_ref, last_recv.at[0])

    for k in (DOWN, UP):
        settle_sent(grad_send.at[0], 4, spread_send.at[k])
    for k in (CARRIED, PENDING, *range(STASH, STASH + TICKS)):
        settle_sent(x_now, PEERS, spread_send.at[k])

    @pl.when(jnp.logical_not(gain_home))
    def _():
        settle(gain_row, spread_send.at[GAIN])

    for t in range(TICKS - 1):
        by_x, by_y = fresh_shift(t)

        @pl.when(by_x + by_y > 0)
        def _():
            settle(relay.at[t], spread_send.at[RELAY + t])

        @pl.when(jnp.logical_not(is_first))
        def _():
            settle(relay.at[t], spread_send.at[FRESH + t])

    for t in range(TICKS):
        for kind, ref in enumerate((f_recv, s_recv, b_recv)):
            settle(ref.at[t], sum_send.at[kind, t])
        for kind, ref in enumerate((f_rows, s_rows, b_rows)):
            settle(ref.at[t, pl.ds(0, YS - 1)], sum_send.at[F_ROWS + kind, t])
        if t < TICKS - 1:
            settle(x_out.at[t], hop_send.at[0, t])
            settle(v_out.at[t], hop_send.at[1, t])
    settle_sent(x_now, PEERS, last_send.at[0])
    settle_sent(grad_send.at[1], 4, last_send.at[3])
    down_ref[...] = owned_grad(0)
    settle(ret_ref, last_recv.at[1])
    settle_sent(x_now, PEERS, last_send.at[1])
    settle_sent(grad_send.at[0], 4, last_send.at[2])


def shards(
    planes,
    carried,
    pending,
    stashed_inputs,
    fresh_batches,
    cotangent,
    norm_gain,
    w_down,
    w_up,
    forward_route,
    backward_route,
):
    row_count, width = carried.shape[2:]
    shard, rank = w_down.shape[1:]
    tokens, columns = row_count // XS, width // YS
    rows = PEERS * tokens
    share = rows // YS

    block = (PEERS, tokens, columns)
    bf16, f32 = jnp.bfloat16, jnp.float32
    dma = pltpu.SemaphoreType.DMA
    in_hbm = pl.BlockSpec(memory_space=pltpu.HBM)
    in_vmem = pl.BlockSpec(memory_space=pltpu.VMEM)
    outgoing, returning, grad_down, grad_up = pl.pallas_call(
        functools.partial(kernel, planes, width),
        out_shape=(
            pltpu.VMEM((row_count, width), bf16),
            pltpu.VMEM((row_count, width), bf16),
            pltpu.VMEM((shard, rank), f32),
            pltpu.VMEM((shard, rank), f32),
        ),
        in_specs=[in_hbm] * 10,
        out_specs=(in_vmem,) * 4,
        scratch_shapes=[
            pltpu.SMEM((2 * (TICKS - 1), PEERS), jnp.int32),
            pltpu.VMEM((1, columns), f32),
            pltpu.SMEM(forward_route.shape, jnp.int32),
            pltpu.SMEM(backward_route.shape, jnp.int32),
            pltpu.VMEM(block, bf16),
            pltpu.VMEM(block, bf16),
            pltpu.VMEM((rows, columns), bf16),
            pltpu.VMEM((TICKS, *block), bf16),
            pltpu.VMEM((TICKS - 1, *block), bf16),
            pltpu.VMEM((TICKS - 1, *block[1:]), bf16),
            (pltpu.VMEM(block, bf16),) * (TICKS - 1),
            (pltpu.VMEM(block, bf16),) * (TICKS - 1),
            pltpu.VMEM((TICKS, *block), bf16),
            pltpu.VMEM((TICKS, *block), bf16),
            pltpu.VMEM((TICKS, YS, share + SPARE, rank), bf16),
            pltpu.VMEM((TICKS, YS - 1, share + SPARE, rank), bf16),
            pltpu.VMEM((TICKS, YS, share + SPARE, rank), bf16),
            pltpu.VMEM((TICKS, YS - 1, share + SPARE, rank), bf16),
            pltpu.VMEM((TICKS, YS, share, rank), bf16),
            pltpu.VMEM((TICKS, YS - 1, share, rank), bf16),
            pltpu.VMEM((TICKS, YS, share, rank), bf16),
            pltpu.VMEM((TICKS, YS, share, rank), bf16),
            pltpu.VMEM((TICKS, YS, share + SPARE, rank), bf16),
            pltpu.VMEM((columns, rank), bf16),
            pltpu.VMEM((columns, rank), bf16),
            pltpu.VMEM((2, columns, rank), f32),
            pltpu.VMEM((2, 4, shard, rank), bf16),
            pltpu.VMEM((2, XS, shard, rank), bf16),
            dma((2,)),
            dma((STASH + TICKS,)),
            dma((STASH + TICKS,)),
            dma((6, TICKS)),
            dma((6, TICKS)),
            dma((2, TICKS - 1)),
            dma((2, TICKS - 1)),
            dma((4,)),
            dma((4,)),
        ],
        compiler_params=pltpu.CompilerParams(
            collective_id=0, has_side_effects=True, vmem_limit_bytes=50 * 1024 * 1024
        ),
    )(*(pltpu.with_memory_space_constraint(a, pltpu.HBM) for a in (
        forward_route,
        backward_route,
        carried[0, 0],
        pending[0, 0],
        stashed_inputs[0, 0],
        fresh_batches[:, 0],
        cotangent[:, 0],
        norm_gain,
        w_down[0],
        w_up[0].T,
    )))
    return outgoing[None, None], returning[None, None], grad_down[None], grad_up.T[None]


def solution(mesh):
    planes = mesh.shape["section"] // 2
    in_specs = (
        P("section", "peer", None, None),
        P("section", "peer", None, None),
        P("section", "peer", None, None, None),
        P(None, "peer", None, None),
        P(None, "peer", None, None),
        P("section", None),
        P("section", "peer", None),
        P("section", None, "peer"),
        P(),
        P(),
    )
    out_specs = (
        P("section", "peer", None, None),
        P("section", "peer", None, None),
        P("section", "peer", None),
        P("section", None, "peer"),
    )
    return jax.shard_map(
        functools.partial(shards, planes), mesh=mesh, in_specs=in_specs, out_specs=out_specs, check_vma=False
    )
```

```python
import functools

import jax
import jax.numpy as jnp
from jax import lax
from jax.experimental import pallas as pl
from jax.experimental.pallas import tpu as pltpu
from jax.sharding import PartitionSpec as P

MESH = pl.DeviceIdType.MESH
NORM_EPS = 1e-05
TICKS = 4
XS = 4
YS = 4
PEERS = 16
LANES = 128
STEP = 256
SPARE = 16

DOWN, CARRIED, UP, PENDING, GAIN, FRESH, RELAY, STASH = 0, 1, 2, 3, 4, 5, 8, 11
F_SUM, S_SUM, B_SUM, F_ROWS, S_ROWS, B_ROWS = range(6)


def iota(shape, dim):
    return lax.broadcasted_iota(jnp.int32, shape, dim)


def to_row(column, first, length):
    shape = (column.shape[0], length)
    return jnp.sum(jnp.where(iota(shape, 1) == iota(shape, 0) + first, column, 0.0), axis=0, keepdims=True)


def to_column(row, first, count):
    shape = (count, row.shape[1])
    return jnp.sum(jnp.where(iota(shape, 1) == iota(shape, 0) + first, row, 0.0), axis=1, keepdims=True)


def in_two(row):
    high = row.astype(jnp.bfloat16).astype(jnp.float32)
    shape = (SPARE, row.shape[1])
    sub = iota(shape, 0)
    return jnp.where(sub == 0, high, jnp.where(sub == 1, row - high, 0.0)).astype(jnp.bfloat16)


def product(a, b, left, right):
    return lax.dot_general(a, b, (((left,), (right,)), ((), ())), preferred_element_type=jnp.float32)


def kernel(
    planes,
    width,
    forward_route,
    backward_route,
    carried,
    pending,
    stash,
    fresh,
    cotangent,
    gain,
    w_down,
    w_up,
    out_ref,
    ret_ref,
    down_ref,
    up_ref,
    inverse,
    gain_row,
    forward_here,
    backward_here,
    x_now,
    v_now,
    u_gained,
    u_all,
    fresh_all,
    relay,
    x_in,
    v_in,
    x_out,
    v_out,
    f_send,
    f_recv,
    s_send,
    s_recv,
    b_send,
    b_recv,
    f_rows,
    s_rows,
    b_rows,
    down_all,
    up_all,
    grad_sum,
    grad_send,
    grad_recv,
    local_sem,
    spread_send,
    spread_recv,
    sum_send,
    sum_recv,
    hop_send,
    hop_recv,
    last_send,
    last_recv,
):
    section = lax.axis_index("section")
    peer = lax.axis_index("peer")
    z, x_hi = section // 2, section % 2
    y, x_lo, core = peer // 4, (peer // 2) % 2, peer % 2
    x = 2 * x_hi + x_lo
    mine = 2 * z + core
    tokens, columns = x_now.shape[1], x_now.shape[2]
    shard, rank = w_down.shape
    rows = PEERS * tokens
    share = rows // YS
    home = core == x_hi
    away = core != x_hi
    is_first = mine == 0
    is_last = mine == 2 * planes - 1
    sends_last = section == 2 * planes - 1

    def place(zz, xx, yy, cc):
        return (2 * zz + xx // 2, 4 * yy + 2 * (xx % 2) + cc)

    def remote(src, dst, send_sem, recv_sem, device):
        pltpu.make_async_remote_copy(
            src_ref=src,
            dst_ref=dst,
            send_sem=send_sem,
            recv_sem=recv_sem,
            device_id=device,
            device_id_type=MESH,
        ).start()

    def settle(ref, sem):
        pltpu.make_async_copy(ref, ref, sem).wait()

    route_copies = [
        pltpu.make_async_copy(route, there, local_sem.at[k])
        for k, (route, there) in enumerate(((forward_route, forward_here), (backward_route, backward_here)))
    ]
    for copy in route_copies:
        copy.start()

    barrier = pltpu.get_barrier_semaphore()
    z_up, z_down = (z + 1) % planes, (z + planes - 1) % planes

    @pl.loop(1, 32)
    def _(i):
        other = (x * 8 + y * 2 + core + i) % 32
        pl.semaphore_signal(
            barrier, inc=1, device_id=place(z, other // 8, (other // 2) % 4, other % 2), device_id_type=MESH
        )

    for zz in (z_up, z_down):
        pl.semaphore_signal(barrier, inc=1, device_id=place(zz, x, y, 1 - core), device_id_type=MESH)


    @pl.when(is_first)
    def _():
        @pl.loop(1, planes)
        def _(i):
            for cc in range(2):
                pl.semaphore_signal(barrier, inc=1, device_id=place(i, x, y, cc), device_id_type=MESH)

    pl.semaphore_wait(barrier, jnp.where(z == 0, 33, 34))

    def cut_of(ref, xx, yy):
        tok = pl.ds(pl.multiple_of(xx * tokens, tokens), tokens)
        col = pl.ds(pl.multiple_of(yy * columns, LANES), columns)
        return ref.at[tok, col] if len(ref.shape) == 2 else ref.at[:, tok, col]

    def spread(source, target, k, first=0, count=XS * YS):
        sems = (spread_send.at[k], spread_recv.at[k])

        if first == 0:

            @pl.when(home)
            def _():
                pltpu.make_async_copy(cut_of(source, x, y), target.at[peer], sems[1]).start()

            @pl.when(away)
            def _():
                remote(cut_of(source, x, y), target.at[peer], *sems, place(z, x, y, x_hi))

        @pl.loop(max(first, 1), first + count)
        def _(i):
            xx, yy = (x + i // YS) % XS, (y + i) % YS
            remote(cut_of(source, xx, yy), target.at[peer], *sems, place(z, xx, yy, x_hi))

    def spread_weight(source, target, k):
        sems = (spread_send.at[k], spread_recv.at[k])
        block = target.at[pl.ds(pl.multiple_of((2 * x_lo + core) * shard, 16), shard)]

        @pl.when(home)
        def _():
            pltpu.make_async_copy(source, block, sems[1]).start()

        @pl.when(away)
        def _():
            remote(source, block, *sems, place(z, x, y, x_hi))

        @pl.loop(1, XS)
        def _(i):
            remote(source, block, *sems, place(z, (x + i) % XS, y, x_hi))

    def settle_sent(ref, count, sem):
        @pl.when(home)
        def _():
            settle(ref.at[pl.ds(0, count - 1)], sem)

        @pl.when(away)
        def _():
            settle(ref.at[pl.ds(0, count)], sem)

    def fresh_shift(t):
        shift = (z + (TICKS - 1) * t) % planes
        return shift // YS, shift % YS

    def relay_fresh(t):
        by_x, by_y = fresh_shift(t)
        xx, yy = 2 * x_hi + (x_lo + by_x) % 2, (y + by_y) % YS
        stays = by_x + by_y == 0

        @pl.when(stays)
        def _():
            pltpu.make_async_copy(cut_of(fresh.at[t], x, y), relay.at[t], spread_recv.at[RELAY + t]).start()

        @pl.when(jnp.logical_not(stays))
        def _():
            remote(
                cut_of(fresh.at[t], xx, yy),
                relay.at[t],
                spread_send.at[RELAY + t],
                spread_recv.at[RELAY + t],
                place(z, xx, yy, core),
            )

    def drop_fresh(t):
        by_x, by_y = fresh_shift(t)
        settle(relay.at[t], spread_recv.at[RELAY + t])
        target = fresh_all.at[t, 4 * ((y + YS - by_y) % YS) + 2 * ((x_lo + 2 - by_x) % 2) + core]

        @pl.when(is_first)
        def _():
            pltpu.make_async_copy(relay.at[t], target, spread_recv.at[FRESH + t]).start()

        @pl.when(jnp.logical_not(is_first))
        def _():
            remote(relay.at[t], target, spread_send.at[FRESH + t], spread_recv.at[FRESH + t], place(0, x, y, 0))

    def spread_stash(t, *parts):
        @pl.when(sends_last)
        def _():
            spread(cotangent.at[t], u_all.at[t], STASH + t, *parts)

        @pl.when(jnp.logical_not(sends_last))
        def _():
            spread(stash.at[t], u_all.at[t], STASH + t, *parts)

    def stash_part(t, part):
        if 0 < t < TICKS - 1:
            if part == 0:
                spread_stash(t + 1)

    gain_home = jnp.logical_and(home, x == 2 * x_lo + core)
    gain_cut = gain.at[:, pl.ds(pl.multiple_of(y * columns, LANES), columns)]

    @pl.when(gain_home)
    def _():
        pltpu.make_async_copy(gain_cut, gain_row, spread_recv.at[GAIN]).start()

    @pl.when(jnp.logical_not(gain_home))
    def _():
        remote(
            gain_cut, gain_row, spread_send.at[GAIN], spread_recv.at[GAIN], place(z, 2 * x_lo + core, y, x_hi)
        )

    for t in range(TICKS - 1):
        relay_fresh(t)
    spread_weight(w_down, down_all, DOWN)
    spread(carried, x_now, CARRIED)
    spread_weight(w_up, up_all, UP)
    spread_stash(0)
    spread(pending, v_now, PENDING)
    for t in range(TICKS - 1):
        drop_fresh(t)

    grad_sum[...] = jnp.zeros_like(grad_sum)

    for copy in route_copies:
        copy.wait()
    boundary = (jnp.maximum(mine - 1, 0), jnp.minimum(mine, 2 * planes - 2))
    for t in range(TICKS - 1):
        for way, route in enumerate((forward_here, backward_here)):
            goes_to = [route[t, boundary[way], q] for q in range(PEERS)]

            @pl.loop(0, PEERS)
            def _(p):
                comes_from = 0
                for q in range(1, PEERS):
                    comes_from = jnp.where(goes_to[q] == p, q, comes_from)
                inverse[way * (TICKS - 1) + t, p] = comes_from

    def flat(value):
        return value.reshape(rows, value.shape[-1])

    def times_gain(value):
        return (value.astype(jnp.float32) * gain_row[...]).astype(jnp.bfloat16)

    def squares_row(value):
        value = value.astype(jnp.float32)
        return in_two(to_row(jnp.sum(value * value, axis=-1, keepdims=True), 0, rows))

    def send_sums(source, target, kind, t):
        for i in range(1, YS):
            yy = (y + i) % YS
            remote(
                source.at[t, yy],
                target.at[t, i - 1],
                sum_send.at[kind, t],
                sum_recv.at[kind, t],
                place(z, x, yy, core),
            )

    def take_sum(source, target, kind, t):
        settle(target.at[t], sum_recv.at[kind, t])
        total = source[t, y].astype(jnp.float32)
        for i in range(YS - 1):
            total = total + target[t, i].astype(jnp.float32)
        return total

    def send_rows(target, kind, t):
        for i in range(1, YS):
            remote(
                target.at[t, y],
                target.at[t, y],
                sum_send.at[kind, t],
                sum_recv.at[kind, t],
                place(z, x, (y + i) % YS, core),
            )

    def take_rows(target, kind, t):
        settle(target.at[t, pl.ds(0, YS - 1)], sum_recv.at[kind, t])

    def scale_of(total):
        squares = to_column(total[share : share + 1] + total[share + 1 : share + 2], y * share, share)
        return lax.rsqrt(squares * (1.0 / width) + NORM_EPS)

    def put_sums(target, t, value):
        target[t, :, 0:share, :] = value.astype(jnp.bfloat16).reshape(YS, share, rank)

    def put_squares(target, t, block):
        for yy in range(YS):
            target[t, yy, share:, :] = block

    def forward_first(t):
        if t == 0:
            settle(down_all, spread_recv.at[DOWN])
            settle(gain_row, spread_recv.at[GAIN])
            settle(x_now, spread_recv.at[CARRIED])
        else:
            settle(x_in[t - 1], hop_recv.at[0, t - 1])

            @pl.when(is_first)
            def _():
                settle(fresh_all.at[t - 1], spread_recv.at[FRESH + t - 1])
                x_now[...] = fresh_all[t - 1]

            @pl.when(jnp.logical_not(is_first))
            def _():
                for p in range(PEERS):
                    x_now[p] = x_in[t - 1][inverse[t - 1, p]]

        stash_part(t - 1, 3)
        x_rows = flat(x_now[...])
        put_sums(f_send, t, product(times_gain(x_rows), down_all[...], 1, 0))
        put_squares(f_send, t, squares_row(x_rows))
        send_sums(f_send, f_recv, F_SUM, t)

    def forward_second(t):
        total = take_sum(f_send, f_recv, F_SUM, t)
        scale = scale_of(total)
        latent = total[0:share] * scale
        f_rows[t, y] = (latent * jax.nn.sigmoid(latent)).astype(jnp.bfloat16)
        send_rows(f_rows, F_ROWS, t)
        return latent, scale

    def forward_third(t):
        if t == 0:
            settle(up_all, spread_recv.at[UP])
        take_rows(f_rows, F_ROWS, t)
        stash_part(t, 1)
        hidden = flat(f_rows[t])
        for start in range(0, columns, STEP):
            cut = slice(start, start + STEP)
            result = flat(x_now[:, :, cut]).astype(jnp.float32) + product(hidden, up_all[cut, :], 1, 1)
            x_out[t, :, :, cut] = result.astype(jnp.bfloat16).reshape(PEERS, tokens, STEP)
            if t < TICKS - 1:
                remote(
                    x_out.at[t, :, :, cut],
                    x_in[t].at[:, :, cut],
                    hop_send.at[0, t],
                    hop_recv.at[0, t],
                    place((z + core) % planes, x, y, 1 - core),
                )
        if t == TICKS - 1:
            to_peers(x_out.at[t], out_ref, 0)

    def stash_first(t):
        settle(u_all.at[t], spread_recv.at[STASH + t])
        u_rows = flat(u_all[t])
        u_gained[...] = times_gain(u_rows)
        put_sums(s_send, t, product(u_gained[...], down_all[...], 1, 0))
        put_squares(s_send, t, squares_row(u_rows))
        send_sums(s_send, s_recv, S_SUM, t)

    def stash_second(t):
        total = take_sum(s_send, s_recv, S_SUM, t)
        scale = scale_of(total)
        latent = total[0:share] * scale
        s_rows[t, y] = (latent * jax.nn.sigmoid(latent)).astype(jnp.bfloat16)
        send_rows(s_rows, S_ROWS, t)
        return latent, scale

    def backward_first(t):
        if t == 0:
            settle(v_now, spread_recv.at[PENDING])
        else:
            settle(v_in[t - 1], hop_recv.at[1, t - 1])
            for p in range(PEERS):
                v_now[p] = v_in[t - 1][inverse[TICKS - 2 + t, p]]

        stash_part(t, 2)

        @pl.when(is_last)
        def _():
            v_now[...] = u_all[t]
            u_all[t] = x_now[...]
            u_gained[...] = times_gain(flat(x_now[...]))

        put_sums(b_send, t, product(flat(v_now[...]), up_all[...], 1, 0))
        send_sums(b_send, b_recv, B_SUM, t)

    def backward_second(t, forward_latent, stash_latent):
        total = take_sum(b_send, b_recv, B_SUM, t)
        latent = jnp.where(is_last, forward_latent[0], stash_latent[0])
        scale = jnp.where(is_last, forward_latent[1], stash_latent[1])
        sigmoid = jax.nn.sigmoid(latent)
        latent_grad = total * sigmoid * (1.0 + latent * (1.0 - sigmoid))
        b_rows[t, y, 0:share, :] = (latent_grad * scale).astype(jnp.bfloat16)
        along = jnp.sum(latent_grad * latent, axis=-1, keepdims=True) * (scale * scale * (1.0 / width))
        b_rows[t, y, share:, :] = in_two(to_row(along, y * share, rows))
        send_rows(b_rows, B_ROWS, t)

    def backward_third(t):
        take_rows(b_rows, B_ROWS, t)
        stash_part(t + 1, 0)
        latent_grad = flat(b_rows[t, :, 0:share, :])
        extra = b_rows[t, :, share:, :].astype(jnp.float32)
        along = to_column(jnp.sum(extra[:, 0:1] + extra[:, 1:2], axis=0), 0, rows)
        for start in range(0, columns, STEP):
            cut = slice(start, start + STEP)
            result = (
                flat(v_now[:, :, cut]).astype(jnp.float32)
                + product(latent_grad, down_all[cut, :], 1, 1) * gain_row[:, cut]
                - flat(u_all[t, :, :, cut]).astype(jnp.float32) * along
            )
            v_out[t, :, :, cut] = result.astype(jnp.bfloat16).reshape(PEERS, tokens, STEP)
            if t < TICKS - 1:
                remote(
                    v_out.at[t, :, :, cut],
                    v_in[t].at[:, :, cut],
                    hop_send.at[1, t],
                    hop_recv.at[1, t],
                    place((z + core + planes - 1) % planes, x, y, 1 - core),
                )
        if t == TICKS - 1:
            to_peers(v_out.at[t], ret_ref, 1)

    def to_peers(source, target, k):
        sems = (last_send.at[k], last_recv.at[k])
        block = cut_of(target, x, y)

        @pl.when(home)
        def _():
            pltpu.make_async_copy(source.at[peer], block, sems[1]).start()

        @pl.when(away)
        def _():
            remote(source.at[peer], block, *sems, (mine, peer))

        @pl.loop(1, PEERS)
        def _(i):
            q = (peer + i) % PEERS
            remote(source.at[q], block, *sems, (mine, q))

    def grad_up(t):
        take_rows(s_rows, S_ROWS, t)
        hidden = jnp.where(is_last, flat(f_rows[t]), flat(s_rows[t]))
        for start in range(0, columns, STEP):
            cut = slice(start, start + STEP)
            grad_sum[1, cut, :] += product(flat(v_now[:, :, cut]), hidden, 0, 0)

    def grad_down(t):
        latent_grad = flat(b_rows[t, :, 0:share, :])
        for start in range(0, columns, STEP):
            cut = slice(start, start + STEP)
            grad_sum[0, cut, :] += product(u_gained[:, cut], latent_grad, 0, 0)

    def to_owners(k):
        for q in range(4):
            grad_send[k, q] = grad_sum[k, q * shard : (q + 1) * shard, :].astype(jnp.bfloat16)
        sems = (last_send.at[2 + k], last_recv.at[2 + k])
        own = 2 * x_lo + core

        @pl.when(home)
        def _():
            pltpu.make_async_copy(grad_send.at[k, own], grad_recv.at[k, x], sems[1]).start()

        @pl.when(away)
        def _():
            remote(grad_send.at[k, own], grad_recv.at[k, x], *sems, (mine, peer))

        @pl.loop(1, 4)
        def _(i):
            q = (own + i) % 4
            remote(grad_send.at[k, q], grad_recv.at[k, x], *sems, (mine, 4 * y + q))

    def owned_grad(k):
        settle(grad_recv.at[k], last_recv.at[2 + k])
        total = grad_recv[k, 0].astype(jnp.float32)
        for i in range(1, XS):
            total = total + grad_recv[k, i].astype(jnp.float32)
        return total

    forward_first(0)
    latent = forward_second(0)
    forward_third(0)
    spread_stash(1)
    stash_first(0)
    for t in range(TICKS - 1):
        backward_first(t)
        forward_first(t + 1)
        stash_latent = stash_second(t)
        backward_second(t, latent, stash_latent)
        latent = forward_second(t + 1)
        grad_up(t)
        backward_third(t)
        forward_third(t + 1)
        grad_down(t)
        stash_first(t + 1)
    last = TICKS - 1
    stash_latent = stash_second(last)
    backward_first(last)
    grad_up(last)
    to_owners(1)
    backward_second(last, latent, stash_latent)
    backward_third(last)
    grad_down(last)
    to_owners(0)

    up_ref[...] = owned_grad(1)
    settle(out_ref, last_recv.at[0])

    for k in (DOWN, UP):
        settle_sent(grad_send.at[0], 4, spread_send.at[k])
    for k in (CARRIED, PENDING, *range(STASH, STASH + TICKS)):
        settle_sent(x_now, PEERS, spread_send.at[k])

    @pl.when(jnp.logical_not(gain_home))
    def _():
        settle(gain_row, spread_send.at[GAIN])

    for t in range(TICKS - 1):
        by_x, by_y = fresh_shift(t)

        @pl.when(by_x + by_y > 0)
        def _():
            settle(relay.at[t], spread_send.at[RELAY + t])

        @pl.when(jnp.logical_not(is_first))
        def _():
            settle(relay.at[t], spread_send.at[FRESH + t])

    for t in range(TICKS):
        for kind, ref in enumerate((f_recv, s_recv, b_recv)):
            settle(ref.at[t], sum_send.at[kind, t])
        for kind, ref in enumerate((f_rows, s_rows, b_rows)):
            settle(ref.at[t, pl.ds(0, YS - 1)], sum_send.at[F_ROWS + kind, t])
        if t < TICKS - 1:
            settle(x_out.at[t], hop_send.at[0, t])
            settle(v_out.at[t], hop_send.at[1, t])
    settle_sent(x_now, PEERS, last_send.at[0])
    settle_sent(grad_send.at[1], 4, last_send.at[3])
    down_ref[...] = owned_grad(0)
    settle(ret_ref, last_recv.at[1])
    settle_sent(x_now, PEERS, last_send.at[1])
    settle_sent(grad_send.at[0], 4, last_send.at[2])


def shards(
    planes,
    carried,
    pending,
    stashed_inputs,
    fresh_batches,
    cotangent,
    norm_gain,
    w_down,
    w_up,
    forward_route,
    backward_route,
):
    row_count, width = carried.shape[2:]
    shard, rank = w_down.shape[1:]
    tokens, columns = row_count // XS, width // YS
    rows = PEERS * tokens
    share = rows // YS

    block = (PEERS, tokens, columns)
    bf16, f32 = jnp.bfloat16, jnp.float32
    dma = pltpu.SemaphoreType.DMA
    in_hbm = pl.BlockSpec(memory_space=pltpu.HBM)
    in_vmem = pl.BlockSpec(memory_space=pltpu.VMEM)
    outgoing, returning, grad_down, grad_up = pl.pallas_call(
        functools.partial(kernel, planes, width),
        out_shape=(
            pltpu.VMEM((row_count, width), bf16),
            pltpu.VMEM((row_count, width), bf16),
            pltpu.VMEM((shard, rank), f32),
            pltpu.VMEM((shard, rank), f32),
        ),
        in_specs=[in_hbm] * 10,
        out_specs=(in_vmem,) * 4,
        scratch_shapes=[
            pltpu.SMEM((2 * (TICKS - 1), PEERS), jnp.int32),
            pltpu.VMEM((1, columns), f32),
            pltpu.SMEM(forward_route.shape, jnp.int32),
            pltpu.SMEM(backward_route.shape, jnp.int32),
            pltpu.VMEM(block, bf16),
            pltpu.VMEM(block, bf16),
            pltpu.VMEM((rows, columns), bf16),
            pltpu.VMEM((TICKS, *block), bf16),
            pltpu.VMEM((TICKS - 1, *block), bf16),
            pltpu.VMEM((TICKS - 1, *block[1:]), bf16),
            (pltpu.VMEM(block, bf16),) * (TICKS - 1),
            (pltpu.VMEM(block, bf16),) * (TICKS - 1),
            pltpu.VMEM((TICKS, *block), bf16),
            pltpu.VMEM((TICKS, *block), bf16),
            pltpu.VMEM((TICKS, YS, share + SPARE, rank), bf16),
            pltpu.VMEM((TICKS, YS - 1, share + SPARE, rank), bf16),
            pltpu.VMEM((TICKS, YS, share + SPARE, rank), bf16),
            pltpu.VMEM((TICKS, YS - 1, share + SPARE, rank), bf16),
            pltpu.VMEM((TICKS, YS, share, rank), bf16),
            pltpu.VMEM((TICKS, YS - 1, share, rank), bf16),
            pltpu.VMEM((TICKS, YS, share, rank), bf16),
            pltpu.VMEM((TICKS, YS, share, rank), bf16),
            pltpu.VMEM((TICKS, YS, share + SPARE, rank), bf16),
            pltpu.VMEM((columns, rank), bf16),
            pltpu.VMEM((columns, rank), bf16),
            pltpu.VMEM((2, columns, rank), f32),
            pltpu.VMEM((2, 4, shard, rank), bf16),
            pltpu.VMEM((2, XS, shard, rank), bf16),
            dma((2,)),
            dma((STASH + TICKS,)),
            dma((STASH + TICKS,)),
            dma((6, TICKS)),
            dma((6, TICKS)),
            dma((2, TICKS - 1)),
            dma((2, TICKS - 1)),
            dma((4,)),
            dma((4,)),
        ],
        compiler_params=pltpu.CompilerParams(
            collective_id=0, has_side_effects=True, vmem_limit_bytes=50 * 1024 * 1024
        ),
    )(*(pltpu.with_memory_space_constraint(a, pltpu.HBM) for a in (
        forward_route,
        backward_route,
        carried[0, 0],
        pending[0, 0],
        stashed_inputs[0, 0],
        fresh_batches[:, 0],
        cotangent[:, 0],
        norm_gain,
        w_down[0],
        w_up[0].T,
    )))
    return outgoing[None, None], returning[None, None], grad_down[None], grad_up.T[None]


def solution(mesh):
    planes = mesh.shape["section"] // 2
    in_specs = (
        P("section", "peer", None, None),
        P("section", "peer", None, None),
        P("section", "peer", None, None, None),
        P(None, "peer", None, None),
        P(None, "peer", None, None),
        P("section", None),
        P("section", "peer", None),
        P("section", None, "peer"),
        P(),
        P(),
    )
    out_specs = (
        P("section", "peer", None, None),
        P("section", "peer", None, None),
        P("section", "peer", None),
        P("section", None, "peer"),
    )
    return jax.shard_map(
        functools.partial(shards, planes), mesh=mesh, in_specs=in_specs, out_specs=out_specs, check_vma=False
    )
```

```python
import functools

import jax
import jax.numpy as jnp
from jax import lax
from jax.experimental import pallas as pl
from jax.experimental.pallas import tpu as pltpu
from jax.sharding import PartitionSpec as P

MESH = pl.DeviceIdType.MESH
NORM_EPS = 1e-05
TICKS = 4
XS = 4
YS = 4
PEERS = 16
LANES = 128
STEP = 256
SPARE = 16

DOWN, CARRIED, UP, PENDING, GAIN, FRESH, RELAY, STASH = 0, 1, 2, 3, 4, 5, 8, 11
F_SUM, S_SUM, B_SUM, F_ROWS, S_ROWS, B_ROWS = range(6)


def iota(shape, dim):
    return lax.broadcasted_iota(jnp.int32, shape, dim)


def to_row(column, first, length):
    shape = (column.shape[0], length)
    return jnp.sum(jnp.where(iota(shape, 1) == iota(shape, 0) + first, column, 0.0), axis=0, keepdims=True)


def to_column(row, first, count):
    shape = (count, row.shape[1])
    return jnp.sum(jnp.where(iota(shape, 1) == iota(shape, 0) + first, row, 0.0), axis=1, keepdims=True)


def in_two(row):
    high = row.astype(jnp.bfloat16).astype(jnp.float32)
    shape = (SPARE, row.shape[1])
    sub = iota(shape, 0)
    return jnp.where(sub == 0, high, jnp.where(sub == 1, row - high, 0.0)).astype(jnp.bfloat16)


def product(a, b, left, right):
    return lax.dot_general(a, b, (((left,), (right,)), ((), ())), preferred_element_type=jnp.float32)


def kernel(
    planes,
    width,
    forward_route,
    backward_route,
    carried,
    pending,
    stash,
    fresh,
    cotangent,
    gain,
    w_down,
    w_up,
    out_ref,
    ret_ref,
    down_ref,
    up_ref,
    inverse,
    gain_row,
    forward_here,
    backward_here,
    x_now,
    v_now,
    u_gained,
    u_all,
    fresh_all,
    relay,
    x_in,
    v_in,
    x_out,
    v_out,
    f_send,
    f_recv,
    s_send,
    s_recv,
    b_send,
    b_recv,
    f_rows,
    s_rows,
    b_rows,
    down_all,
    up_all,
    grad_sum,
    grad_send,
    grad_recv,
    local_sem,
    spread_send,
    spread_recv,
    sum_send,
    sum_recv,
    hop_send,
    hop_recv,
    last_send,
    last_recv,
):
    section = lax.axis_index("section")
    peer = lax.axis_index("peer")
    z, x_hi = section // 2, section % 2
    y, x_lo, core = peer // 4, (peer // 2) % 2, peer % 2
    x = 2 * x_hi + x_lo
    mine = 2 * z + core
    tokens, columns = x_now.shape[1], x_now.shape[2]
    shard, rank = w_down.shape
    rows = PEERS * tokens
    share = rows // YS
    home = core == x_hi
    away = core != x_hi
    is_first = mine == 0
    is_last = mine == 2 * planes - 1
    sends_last = section == 2 * planes - 1

    def place(zz, xx, yy, cc):
        return (2 * zz + xx // 2, 4 * yy + 2 * (xx % 2) + cc)

    def remote(src, dst, send_sem, recv_sem, device):
        pltpu.make_async_remote_copy(
            src_ref=src,
            dst_ref=dst,
            send_sem=send_sem,
            recv_sem=recv_sem,
            device_id=device,
            device_id_type=MESH,
        ).start()

    def settle(ref, sem):
        pltpu.make_async_copy(ref, ref, sem).wait()

    route_copies = [
        pltpu.make_async_copy(route, there, local_sem.at[k])
        for k, (route, there) in enumerate(((forward_route, forward_here), (backward_route, backward_here)))
    ]
    for copy in route_copies:
        copy.start()

    barrier = pltpu.get_barrier_semaphore()
    z_up, z_down = (z + 1) % planes, (z + planes - 1) % planes

    @pl.loop(1, 32)
    def _(i):
        other = (x * 8 + y * 2 + core + i) % 32
        pl.semaphore_signal(
            barrier, inc=1, device_id=place(z, other // 8, (other // 2) % 4, other % 2), device_id_type=MESH
        )

    for zz in (z_up, z_down):
        pl.semaphore_signal(barrier, inc=1, device_id=place(zz, x, y, 1 - core), device_id_type=MESH)


    @pl.when(is_first)
    def _():
        @pl.loop(1, planes)
        def _(i):
            for cc in range(2):
                pl.semaphore_signal(barrier, inc=1, device_id=place(i, x, y, cc), device_id_type=MESH)

    pl.semaphore_wait(barrier, jnp.where(z == 0, 33, 34))

    def cut_of(ref, xx, yy):
        tok = pl.ds(pl.multiple_of(xx * tokens, tokens), tokens)
        col = pl.ds(pl.multiple_of(yy * columns, LANES), columns)
        return ref.at[tok, col] if len(ref.shape) == 2 else ref.at[:, tok, col]

    def spread(source, target, k, first=0, count=XS * YS):
        sems = (spread_send.at[k], spread_recv.at[k])

        if first == 0:

            @pl.when(home)
            def _():
                pltpu.make_async_copy(cut_of(source, x, y), target.at[peer], sems[1]).start()

            @pl.when(away)
            def _():
                remote(cut_of(source, x, y), target.at[peer], *sems, place(z, x, y, x_hi))

        @pl.loop(max(first, 1), first + count)
        def _(i):
            xx, yy = (x + i) % XS, (y + i // XS + i) % YS
            remote(cut_of(source, xx, yy), target.at[peer], *sems, place(z, xx, yy, x_hi))

    def spread_weight(source, target, k):
        sems = (spread_send.at[k], spread_recv.at[k])
        block = target.at[pl.ds(pl.multiple_of((2 * x_lo + core) * shard, 16), shard)]

        @pl.when(home)
        def _():
            pltpu.make_async_copy(source, block, sems[1]).start()

        @pl.when(away)
        def _():
            remote(source, block, *sems, place(z, x, y, x_hi))

        @pl.loop(1, XS)
        def _(i):
            remote(source, block, *sems, place(z, (x + i) % XS, y, x_hi))

    def settle_sent(ref, count, sem):
        @pl.when(home)
        def _():
            settle(ref.at[pl.ds(0, count - 1)], sem)

        @pl.when(away)
        def _():
            settle(ref.at[pl.ds(0, count)], sem)

    def fresh_shift(t):
        shift = (z + (TICKS - 1) * t) % planes
        return shift // YS, shift % YS

    def relay_fresh(t):
        by_x, by_y = fresh_shift(t)
        xx, yy = 2 * x_hi + (x_lo + by_x) % 2, (y + by_y) % YS
        stays = by_x + by_y == 0

        @pl.when(stays)
        def _():
            pltpu.make_async_copy(cut_of(fresh.at[t], x, y), relay.at[t], spread_recv.at[RELAY + t]).start()

        @pl.when(jnp.logical_not(stays))
        def _():
            remote(
                cut_of(fresh.at[t], xx, yy),
                relay.at[t],
                spread_send.at[RELAY + t],
                spread_recv.at[RELAY + t],
                place(z, xx, yy, core),
            )

    def drop_fresh(t):
        by_x, by_y = fresh_shift(t)
        settle(relay.at[t], spread_recv.at[RELAY + t])
        target = fresh_all.at[t, 4 * ((y + YS - by_y) % YS) + 2 * ((x_lo + 2 - by_x) % 2) + core]

        @pl.when(is_first)
        def _():
            pltpu.make_async_copy(relay.at[t], target, spread_recv.at[FRESH + t]).start()

        @pl.when(jnp.logical_not(is_first))
        def _():
            remote(relay.at[t], target, spread_send.at[FRESH + t], spread_recv.at[FRESH + t], place(0, x, y, 0))

    def spread_stash(t, *parts):
        @pl.when(sends_last)
        def _():
            spread(cotangent.at[t], u_all.at[t], STASH + t, *parts)

        @pl.when(jnp.logical_not(sends_last))
        def _():
            spread(stash.at[t], u_all.at[t], STASH + t, *parts)

    def stash_part(t, part):
        if 0 < t < TICKS - 1:
            if part == 0:
                spread_stash(t + 1)

    gain_home = jnp.logical_and(home, x == 2 * x_lo + core)
    gain_cut = gain.at[:, pl.ds(pl.multiple_of(y * columns, LANES), columns)]

    @pl.when(gain_home)
    def _():
        pltpu.make_async_copy(gain_cut, gain_row, spread_recv.at[GAIN]).start()

    @pl.when(jnp.logical_not(gain_home))
    def _():
        remote(
            gain_cut, gain_row, spread_send.at[GAIN], spread_recv.at[GAIN], place(z, 2 * x_lo + core, y, x_hi)
        )

    for t in range(TICKS - 1):
        relay_fresh(t)
    spread_weight(w_down, down_all, DOWN)
    spread(carried, x_now, CARRIED)
    spread_weight(w_up, up_all, UP)
    spread_stash(0)
    spread(pending, v_now, PENDING)
    for t in range(TICKS - 1):
        drop_fresh(t)

    grad_sum[...] = jnp.zeros_like(grad_sum)

    for copy in route_copies:
        copy.wait()
    boundary = (jnp.maximum(mine - 1, 0), jnp.minimum(mine, 2 * planes - 2))
    for t in range(TICKS - 1):
        for way, route in enumerate((forward_here, backward_here)):
            goes_to = [route[t, boundary[way], q] for q in range(PEERS)]

            @pl.loop(0, PEERS)
            def _(p):
                comes_from = 0
                for q in range(1, PEERS):
                    comes_from = jnp.where(goes_to[q] == p, q, comes_from)
                inverse[way * (TICKS - 1) + t, p] = comes_from

    def flat(value):
        return value.reshape(rows, value.shape[-1])

    def times_gain(value):
        return (value.astype(jnp.float32) * gain_row[...]).astype(jnp.bfloat16)

    def squares_row(value):
        value = value.astype(jnp.float32)
        return in_two(to_row(jnp.sum(value * value, axis=-1, keepdims=True), 0, rows))

    def send_sums(source, target, kind, t):
        for i in range(1, YS):
            yy = (y + i) % YS
            remote(
                source.at[t, yy],
                target.at[t, i - 1],
                sum_send.at[kind, t],
                sum_recv.at[kind, t],
                place(z, x, yy, core),
            )

    def take_sum(source, target, kind, t):
        settle(target.at[t], sum_recv.at[kind, t])
        total = source[t, y].astype(jnp.float32)
        for i in range(YS - 1):
            total = total + target[t, i].astype(jnp.float32)
        return total

    def send_rows(target, kind, t):
        for i in range(1, YS):
            remote(
                target.at[t, y],
                target.at[t, y],
                sum_send.at[kind, t],
                sum_recv.at[kind, t],
                place(z, x, (y + i) % YS, core),
            )

    def take_rows(target, kind, t):
        settle(target.at[t, pl.ds(0, YS - 1)], sum_recv.at[kind, t])

    def scale_of(total):
        squares = to_column(total[share : share + 1] + total[share + 1 : share + 2], y * share, share)
        return lax.rsqrt(squares * (1.0 / width) + NORM_EPS)

    def put_sums(target, t, value):
        target[t, :, 0:share, :] = value.astype(jnp.bfloat16).reshape(YS, share, rank)

    def put_squares(target, t, block):
        for yy in range(YS):
            target[t, yy, share:, :] = block

    def forward_first(t):
        if t == 0:
            settle(down_all, spread_recv.at[DOWN])
            settle(gain_row, spread_recv.at[GAIN])
            settle(x_now, spread_recv.at[CARRIED])
        else:
            settle(x_in[t - 1], hop_recv.at[0, t - 1])

            @pl.when(is_first)
            def _():
                settle(fresh_all.at[t - 1], spread_recv.at[FRESH + t - 1])
                x_now[...] = fresh_all[t - 1]

            @pl.when(jnp.logical_not(is_first))
            def _():
                for p in range(PEERS):
                    x_now[p] = x_in[t - 1][inverse[t - 1, p]]

        stash_part(t - 1, 3)
        x_rows = flat(x_now[...])
        put_sums(f_send, t, product(times_gain(x_rows), down_all[...], 1, 0))
        put_squares(f_send, t, squares_row(x_rows))
        send_sums(f_send, f_recv, F_SUM, t)

    def forward_second(t):
        total = take_sum(f_send, f_recv, F_SUM, t)
        scale = scale_of(total)
        latent = total[0:share] * scale
        f_rows[t, y] = (latent * jax.nn.sigmoid(latent)).astype(jnp.bfloat16)
        send_rows(f_rows, F_ROWS, t)
        return latent, scale

    def forward_third(t):
        if t == 0:
            settle(up_all, spread_recv.at[UP])
        take_rows(f_rows, F_ROWS, t)
        stash_part(t, 1)
        hidden = flat(f_rows[t])
        for start in range(0, columns, STEP):
            cut = slice(start, start + STEP)
            result = flat(x_now[:, :, cut]).astype(jnp.float32) + product(hidden, up_all[cut, :], 1, 1)
            x_out[t, :, :, cut] = result.astype(jnp.bfloat16).reshape(PEERS, tokens, STEP)
            if t < TICKS - 1:
                remote(
                    x_out.at[t, :, :, cut],
                    x_in[t].at[:, :, cut],
                    hop_send.at[0, t],
                    hop_recv.at[0, t],
                    place((z + core) % planes, x, y, 1 - core),
                )
        if t == TICKS - 1:
            to_peers(x_out.at[t], out_ref, 0)

    def stash_first(t):
        settle(u_all.at[t], spread_recv.at[STASH + t])
        u_rows = flat(u_all[t])
        u_gained[...] = times_gain(u_rows)
        put_sums(s_send, t, product(u_gained[...], down_all[...], 1, 0))
        put_squares(s_send, t, squares_row(u_rows))
        send_sums(s_send, s_recv, S_SUM, t)

    def stash_second(t):
        total = take_sum(s_send, s_recv, S_SUM, t)
        scale = scale_of(total)
        latent = total[0:share] * scale
        s_rows[t, y] = (latent * jax.nn.sigmoid(latent)).astype(jnp.bfloat16)
        send_rows(s_rows, S_ROWS, t)
        return latent, scale

    def backward_first(t):
        if t == 0:
            settle(v_now, spread_recv.at[PENDING])
        else:
            settle(v_in[t - 1], hop_recv.at[1, t - 1])
            for p in range(PEERS):
                v_now[p] = v_in[t - 1][inverse[TICKS - 2 + t, p]]

        stash_part(t, 2)

        @pl.when(is_last)
        def _():
            v_now[...] = u_all[t]
            u_all[t] = x_now[...]
            u_gained[...] = times_gain(flat(x_now[...]))

        put_sums(b_send, t, product(flat(v_now[...]), up_all[...], 1, 0))
        send_sums(b_send, b_recv, B_SUM, t)

    def backward_second(t, forward_latent, stash_latent):
        total = take_sum(b_send, b_recv, B_SUM, t)
        latent = jnp.where(is_last, forward_latent[0], stash_latent[0])
        scale = jnp.where(is_last, forward_latent[1], stash_latent[1])
        sigmoid = jax.nn.sigmoid(latent)
        latent_grad = total * sigmoid * (1.0 + latent * (1.0 - sigmoid))
        b_rows[t, y, 0:share, :] = (latent_grad * scale).astype(jnp.bfloat16)
        along = jnp.sum(latent_grad * latent, axis=-1, keepdims=True) * (scale * scale * (1.0 / width))
        b_rows[t, y, share:, :] = in_two(to_row(along, y * share, rows))
        send_rows(b_rows, B_ROWS, t)

    def backward_third(t):
        take_rows(b_rows, B_ROWS, t)
        stash_part(t + 1, 0)
        latent_grad = flat(b_rows[t, :, 0:share, :])
        extra = b_rows[t, :, share:, :].astype(jnp.float32)
        along = to_column(jnp.sum(extra[:, 0:1] + extra[:, 1:2], axis=0), 0, rows)
        for start in range(0, columns, STEP):
            cut = slice(start, start + STEP)
            result = (
                flat(v_now[:, :, cut]).astype(jnp.float32)
                + product(latent_grad, down_all[cut, :], 1, 1) * gain_row[:, cut]
                - flat(u_all[t, :, :, cut]).astype(jnp.float32) * along
            )
            v_out[t, :, :, cut] = result.astype(jnp.bfloat16).reshape(PEERS, tokens, STEP)
            if t < TICKS - 1:
                remote(
                    v_out.at[t, :, :, cut],
                    v_in[t].at[:, :, cut],
                    hop_send.at[1, t],
                    hop_recv.at[1, t],
                    place((z + core + planes - 1) % planes, x, y, 1 - core),
                )
        if t == TICKS - 1:
            to_peers(v_out.at[t], ret_ref, 1)

    def to_peers(source, target, k):
        sems = (last_send.at[k], last_recv.at[k])
        block = cut_of(target, x, y)

        @pl.when(home)
        def _():
            pltpu.make_async_copy(source.at[peer], block, sems[1]).start()

        @pl.when(away)
        def _():
            remote(source.at[peer], block, *sems, (mine, peer))

        @pl.loop(1, PEERS)
        def _(i):
            q = (peer + i) % PEERS
            remote(source.at[q], block, *sems, (mine, q))

    def grad_up(t):
        take_rows(s_rows, S_ROWS, t)
        hidden = jnp.where(is_last, flat(f_rows[t]), flat(s_rows[t]))
        for start in range(0, columns, STEP):
            cut = slice(start, start + STEP)
            grad_sum[1, cut, :] += product(flat(v_now[:, :, cut]), hidden, 0, 0)

    def grad_down(t):
        latent_grad = flat(b_rows[t, :, 0:share, :])
        for start in range(0, columns, STEP):
            cut = slice(start, start + STEP)
            grad_sum[0, cut, :] += product(u_gained[:, cut], latent_grad, 0, 0)

    def to_owners(k):
        for q in range(4):
            grad_send[k, q] = grad_sum[k, q * shard : (q + 1) * shard, :].astype(jnp.bfloat16)
        sems = (last_send.at[2 + k], last_recv.at[2 + k])
        own = 2 * x_lo + core

        @pl.when(home)
        def _():
            pltpu.make_async_copy(grad_send.at[k, own], grad_recv.at[k, x], sems[1]).start()

        @pl.when(away)
        def _():
            remote(grad_send.at[k, own], grad_recv.at[k, x], *sems, (mine, peer))

        @pl.loop(1, 4)
        def _(i):
            q = (own + i) % 4
            remote(grad_send.at[k, q], grad_recv.at[k, x], *sems, (mine, 4 * y + q))

    def owned_grad(k):
        settle(grad_recv.at[k], last_recv.at[2 + k])
        total = grad_recv[k, 0].astype(jnp.float32)
        for i in range(1, XS):
            total = total + grad_recv[k, i].astype(jnp.float32)
        return total

    forward_first(0)
    latent = forward_second(0)
    forward_third(0)
    spread_stash(1)
    stash_first(0)
    for t in range(TICKS - 1):
        backward_first(t)
        forward_first(t + 1)
        stash_latent = stash_second(t)
        backward_second(t, latent, stash_latent)
        latent = forward_second(t + 1)
        grad_up(t)
        backward_third(t)
        forward_third(t + 1)
        grad_down(t)
        stash_first(t + 1)
    last = TICKS - 1
    stash_latent = stash_second(last)
    backward_first(last)
    grad_up(last)
    to_owners(1)
    backward_second(last, latent, stash_latent)
    backward_third(last)
    grad_down(last)
    to_owners(0)

    up_ref[...] = owned_grad(1)
    settle(out_ref, last_recv.at[0])

    for k in (DOWN, UP):
        settle_sent(grad_send.at[0], 4, spread_send.at[k])
    for k in (CARRIED, PENDING, *range(STASH, STASH + TICKS)):
        settle_sent(x_now, PEERS, spread_send.at[k])

    @pl.when(jnp.logical_not(gain_home))
    def _():
        settle(gain_row, spread_send.at[GAIN])

    for t in range(TICKS - 1):
        by_x, by_y = fresh_shift(t)

        @pl.when(by_x + by_y > 0)
        def _():
            settle(relay.at[t], spread_send.at[RELAY + t])

        @pl.when(jnp.logical_not(is_first))
        def _():
            settle(relay.at[t], spread_send.at[FRESH + t])

    for t in range(TICKS):
        for kind, ref in enumerate((f_recv, s_recv, b_recv)):
            settle(ref.at[t], sum_send.at[kind, t])
        for kind, ref in enumerate((f_rows, s_rows, b_rows)):
            settle(ref.at[t, pl.ds(0, YS - 1)], sum_send.at[F_ROWS + kind, t])
        if t < TICKS - 1:
            settle(x_out.at[t], hop_send.at[0, t])
            settle(v_out.at[t], hop_send.at[1, t])
    settle_sent(x_now, PEERS, last_send.at[0])
    settle_sent(grad_send.at[1], 4, last_send.at[3])
    down_ref[...] = owned_grad(0)
    settle(ret_ref, last_recv.at[1])
    settle_sent(x_now, PEERS, last_send.at[1])
    settle_sent(grad_send.at[0], 4, last_send.at[2])


def shards(
    planes,
    carried,
    pending,
    stashed_inputs,
    fresh_batches,
    cotangent,
    norm_gain,
    w_down,
    w_up,
    forward_route,
    backward_route,
):
    row_count, width = carried.shape[2:]
    shard, rank = w_down.shape[1:]
    tokens, columns = row_count // XS, width // YS
    rows = PEERS * tokens
    share = rows // YS

    block = (PEERS, tokens, columns)
    bf16, f32 = jnp.bfloat16, jnp.float32
    dma = pltpu.SemaphoreType.DMA
    in_hbm = pl.BlockSpec(memory_space=pltpu.HBM)
    in_vmem = pl.BlockSpec(memory_space=pltpu.VMEM)
    outgoing, returning, grad_down, grad_up = pl.pallas_call(
        functools.partial(kernel, planes, width),
        out_shape=(
            pltpu.VMEM((row_count, width), bf16),
            pltpu.VMEM((row_count, width), bf16),
            pltpu.VMEM((shard, rank), f32),
            pltpu.VMEM((shard, rank), f32),
        ),
        in_specs=[in_hbm] * 10,
        out_specs=(in_vmem,) * 4,
        scratch_shapes=[
            pltpu.SMEM((2 * (TICKS - 1), PEERS), jnp.int32),
            pltpu.VMEM((1, columns), f32),
            pltpu.SMEM(forward_route.shape, jnp.int32),
            pltpu.SMEM(backward_route.shape, jnp.int32),
            pltpu.VMEM(block, bf16),
            pltpu.VMEM(block, bf16),
            pltpu.VMEM((rows, columns), bf16),
            pltpu.VMEM((TICKS, *block), bf16),
            pltpu.VMEM((TICKS - 1, *block), bf16),
            pltpu.VMEM((TICKS - 1, *block[1:]), bf16),
            (pltpu.VMEM(block, bf16),) * (TICKS - 1),
            (pltpu.VMEM(block, bf16),) * (TICKS - 1),
            pltpu.VMEM((TICKS, *block), bf16),
            pltpu.VMEM((TICKS, *block), bf16),
            pltpu.VMEM((TICKS, YS, share + SPARE, rank), bf16),
            pltpu.VMEM((TICKS, YS - 1, share + SPARE, rank), bf16),
            pltpu.VMEM((TICKS, YS, share + SPARE, rank), bf16),
            pltpu.VMEM((TICKS, YS - 1, share + SPARE, rank), bf16),
            pltpu.VMEM((TICKS, YS, share, rank), bf16),
            pltpu.VMEM((TICKS, YS - 1, share, rank), bf16),
            pltpu.VMEM((TICKS, YS, share, rank), bf16),
            pltpu.VMEM((TICKS, YS, share, rank), bf16),
            pltpu.VMEM((TICKS, YS, share + SPARE, rank), bf16),
            pltpu.VMEM((columns, rank), bf16),
            pltpu.VMEM((columns, rank), bf16),
            pltpu.VMEM((2, columns, rank), f32),
            pltpu.VMEM((2, 4, shard, rank), bf16),
            pltpu.VMEM((2, XS, shard, rank), bf16),
            dma((2,)),
            dma((STASH + TICKS,)),
            dma((STASH + TICKS,)),
            dma((6, TICKS)),
            dma((6, TICKS)),
            dma((2, TICKS - 1)),
            dma((2, TICKS - 1)),
            dma((4,)),
            dma((4,)),
        ],
        compiler_params=pltpu.CompilerParams(
            collective_id=0, has_side_effects=True, vmem_limit_bytes=50 * 1024 * 1024
        ),
    )(*(pltpu.with_memory_space_constraint(a, pltpu.HBM) for a in (
        forward_route,
        backward_route,
        carried[0, 0],
        pending[0, 0],
        stashed_inputs[0, 0],
        fresh_batches[:, 0],
        cotangent[:, 0],
        norm_gain,
        w_down[0],
        w_up[0].T,
    )))
    return outgoing[None, None], returning[None, None], grad_down[None], grad_up.T[None]


def solution(mesh):
    planes = mesh.shape["section"] // 2
    in_specs = (
        P("section", "peer", None, None),
        P("section", "peer", None, None),
        P("section", "peer", None, None, None),
        P(None, "peer", None, None),
        P(None, "peer", None, None),
        P("section", None),
        P("section", "peer", None),
        P("section", None, "peer"),
        P(),
        P(),
    )
    out_specs = (
        P("section", "peer", None, None),
        P("section", "peer", None, None),
        P("section", "peer", None),
        P("section", None, "peer"),
    )
    return jax.shard_map(
        functools.partial(shards, planes), mesh=mesh, in_specs=in_specs, out_specs=out_specs, check_vma=False
    )
```
